32 devices in a mesh: dp: 4 (over y, x), ctx: 2 (over core), ch: 4 (over z).
Axes of the slice: x: 2, y: 2, z: 4, core: 2. Of those that a mesh axis runs over, the one named last changes fastest.
Arguments:
- gate_input: bfloat16 [4, 256, 4096], P('dp', 'ctx', 'ch'), may hold values from -6 to 6
- conv_input: bfloat16 [4, 256, 4096], P('dp', 'ctx', 'ch'), may hold values from -6 to 6
- grad_output: bfloat16 [4, 256, 4096], P('dp', 'ctx', 'ch'), may hold values from -6 to 6
- kernel: bfloat16 [128, 256], P('ch'), may hold values from -0.375 to 0.375
Outputs:
- output: bfloat16 [4, 256, 4096], P('dp', 'ctx', 'ch')
- grad_gate: bfloat16 [4, 256, 4096], P('dp', 'ctx', 'ch')
- grad_conv: bfloat16 [4, 256, 4096], P('dp', 'ctx', 'ch')
- grad_kernel: float32 [128, 256], P('ch', ('dp', 'ctx'))
The draws below stay inside these ranges and needn't reach their ends.
All inputs are finite; a program needn't handle non-finite values.
Results may differ from the reference program's by a relative error of at most 0.0049.
Values may be sent and summed in bfloat16 or wider, within the bound.
A program may use at most 64 MiB of HBM per device.

```python
import math
import jax
import jax.numpy as jnp
from jax import lax

D = 4096
GROUP = 32
FG = 128
TOK_DEV = 128
LAG_BLOCKS = 2
LAGS = 256
SEQ = 256
SEQS = 4
N_CTX = 2


def shard_levels(key, shape, split, least, high):
    def one(dim, parts):
        heights = jax.random.uniform(jax.random.fold_in(jax.random.fold_in(key, 6), dim), (parts,), jnp.float32, least / len(split), high / len(split))
        return jnp.repeat(jnp.exp(heights), shape[dim] // parts).reshape((-1,) + (1,) * (len(shape) - dim - 1))

    loudness = one(*split[0])
    for cut in split[1:]:
        loudness = loudness * one(*cut)
    return loudness


def normal_values(key, shape, deviation, bound, pieces=(), kind=jnp.bfloat16):
    values = jax.random.normal(key, shape, jnp.float32) * deviation
    if len(pieces) > 0:
        values = shard_levels(key, shape, pieces, -0.22, 0.18) * values
    return jnp.clip(values, min=-bound, max=bound).astype(kind)


def setup_inputs(seed: int = 0) -> dict:
    keys = jax.random.split(jax.random.key(seed), 5)
    gate_input = normal_values(keys[0], (SEQS, SEQ, D), 1.0, 6.0, ((0, 4), (1, 2), (2, 4)))
    conv_input = normal_values(keys[1], (SEQS, SEQ, D), 1.0, 6.0, ((0, 4), (1, 2), (2, 4)))
    grad_output = normal_values(keys[2], (SEQS, SEQ, D), 1.0, 6.0, ((0, 4), (1, 2), (2, 4)))
    kernel = normal_values(keys[3], (FG, LAGS), LAGS ** -0.5, 0.375, ((0, 4),))
    return dict(gate_input=gate_input, conv_input=conv_input, grad_output=grad_output, kernel=kernel)


def toeplitz(kernel, offset):
    positions = jnp.arange(TOK_DEV, dtype=jnp.int32)
    indices = offset.astype(jnp.int32) * TOK_DEV + positions[:, None] - positions[None, :]
    lagged = jnp.take(kernel, jnp.clip(indices, 0, LAGS - 1), axis=1)
    valid = (indices >= 0) & (indices < LAGS)
    return jnp.where(valid[None], lagged, jnp.zeros_like(lagged))

def diagonal_sums(matrix):
    groups = matrix.shape[0]
    extent = matrix.shape[1]
    flipped = matrix[:, :, ::-1]
    padded = jnp.pad(flipped, ((0, 0), (0, 0), (0, extent)))
    flattened = padded.reshape(groups, 2 * extent * extent)[:, :extent * (2 * extent - 1)]
    totals = lax.optimization_barrier(jnp.sum(flattened.reshape(groups, extent, 2 * extent - 1).astype(jnp.float32), axis=1))
    return jnp.pad(totals, ((0, 0), (0, 1)))

def reference(gate_input, conv_input, grad_output, kernel):

    def forward_block(offset, block):
        matrix = toeplitz(kernel, offset).astype(jnp.float32)
        shaped = block.astype(jnp.float32).reshape(TOK_DEV, FG, GROUP)
        return jnp.einsum('gab,bgc->agc', matrix, shaped).reshape(TOK_DEV, D)

    def backward_block(offset, block):
        matrix = toeplitz(kernel, offset).astype(jnp.float32)
        shaped = block.astype(jnp.float32).reshape(TOK_DEV, FG, GROUP)
        return jnp.einsum('gab,agc->bgc', matrix, shaped).reshape(TOK_DEV, D)

    def pair_block(grad_block, value_block):
        left_side = grad_block.astype(jnp.float32).reshape(TOK_DEV, FG, GROUP)
        right_side = value_block.astype(jnp.float32).reshape(TOK_DEV, FG, GROUP)
        return jnp.einsum('agc,bgc->gab', left_side, right_side).astype(jnp.bfloat16)
    block_ids = jnp.arange(N_CTX, dtype=jnp.int32)
    offset_ids = jnp.arange(LAG_BLOCKS + 1, dtype=jnp.int32)

    def one_sample(inputs):
        gate_rows, value_rows, grad_rows = inputs
        value_blocks = value_rows.reshape(N_CTX, TOK_DEV, D)

        def forward_row(target):

            def add_term(source, running):
                return running + forward_block(target - source, value_blocks[source])
            first = jnp.maximum(target - LAG_BLOCKS, 0).astype(jnp.int32)
            return lax.fori_loop(first, target + 1, add_term, jnp.zeros((TOK_DEV, D), jnp.float32))
        convolved = lax.map(forward_row, block_ids).reshape(SEQ, D)
        output = (gate_rows.astype(jnp.float32) * convolved).astype(jnp.bfloat16)
        grad_mixed = (gate_rows.astype(jnp.float32) * grad_rows.astype(jnp.float32)).astype(jnp.bfloat16)
        grad_gate = (grad_rows.astype(jnp.float32) * convolved).astype(jnp.bfloat16)
        grad_blocks = grad_mixed.reshape(N_CTX, TOK_DEV, D)

        def backward_row(source):

            def add_term(target, running):
                return running + backward_block(target - source, grad_blocks[target])
            last = jnp.minimum(source + LAG_BLOCKS + 1, N_CTX).astype(jnp.int32)
            return lax.fori_loop(source, last, add_term, jnp.zeros((TOK_DEV, D), jnp.float32))
        grad_conv = lax.map(backward_row, block_ids).reshape(SEQ, D).astype(jnp.bfloat16)

        def lag_window(offset):

            def add_pair(target, running):
                return running + pair_block(grad_blocks[target], value_blocks[target - offset]).astype(jnp.float32)
            summed = lax.fori_loop(offset, jnp.int32(N_CTX), add_pair, jnp.zeros((FG, TOK_DEV, TOK_DEV), jnp.float32))
            return diagonal_sums(summed)
        windows = lax.map(lag_window, offset_ids)
        return (output, grad_gate, grad_conv, windows)
    output, grad_gate, grad_conv, windows = lax.map(one_sample, (gate_input, conv_input, grad_output))
    windows = lax.optimization_barrier(jnp.sum(windows, axis=0))
    first_half = windows[:, :, :TOK_DEV]
    second_half = windows[:, :, TOK_DEV:]
    zero_block = jnp.zeros((1, FG, TOK_DEV), jnp.float32)
    stacked = jnp.concatenate([first_half, zero_block], axis=0) + jnp.concatenate([zero_block, second_half], axis=0)
    buffer = jnp.transpose(stacked, (1, 0, 2)).reshape(FG, (LAG_BLOCKS + 2) * TOK_DEV)
    grad_kernel = buffer[:, TOK_DEV - 1:TOK_DEV - 1 + LAGS] / math.sqrt(SEQS * SEQ)
    return (output, grad_gate, grad_conv, grad_kernel)
```

```python
import functools
import math

import jax
import jax.numpy as jnp
from jax import lax
from jax.experimental import pallas as pl
from jax.experimental.pallas import tpu as pltpu
from jax.sharding import PartitionSpec as P


def toeplitz(padded_kernel, offset, tok_rows):
    groups = padded_kernel.shape[0]
    segment = lax.dynamic_slice_in_dim(padded_kernel, offset * tok_rows + 1, 2 * tok_rows, 1)
    reverse = segment[:, ::-1]
    rolled = jnp.concatenate([reverse[:, tok_rows:], reverse[:, :tok_rows]], axis=1)
    tiled = jnp.tile(rolled, (1, tok_rows))[:, : tok_rows * (2 * tok_rows - 1)]
    return tiled.reshape(groups, tok_rows, 2 * tok_rows - 1)[:, :, :tok_rows]


def diagonal_sums(matrix):
    groups = matrix.shape[0]
    extent = matrix.shape[1]
    flipped = matrix[:, :, ::-1]
    padded = jnp.pad(flipped, ((0, 0), (0, 0), (0, extent)))
    flattened = padded.reshape(groups, 2 * extent * extent)[:, : extent * (2 * extent - 1)]
    totals = jnp.sum(flattened.reshape(groups, extent, 2 * extent - 1), axis=1, dtype=jnp.float32)
    return jnp.pad(totals, ((0, 0), (0, 1)))


def general_body(gate_input, conv_input, grad_output, kernel):
    tok_rows = gate_input.shape[1]
    channels = gate_input.shape[2]
    groups = kernel.shape[0]
    group_size = channels // groups
    lag_count = kernel.shape[1]
    lag_blocks = lag_count // tok_rows
    padded_kernel = jnp.pad(kernel, ((0, 0), (tok_rows, 2 * tok_rows)))
    blocks = lax.axis_size("ctx")
    own_block = lax.axis_index("ctx")
    gate_rows = gate_input[0]
    grad_rows = grad_output[0]
    grad_mixed = (gate_rows.astype(jnp.float32) * grad_rows.astype(jnp.float32)).astype(
        jnp.bfloat16
    )

    def forward_add(running, matrix, block):
        shaped = block.reshape(tok_rows, groups, group_size)
        return running + jnp.einsum(
            "gab,bgc->agc", matrix, shaped, preferred_element_type=jnp.float32
        ).reshape(tok_rows, channels)

    def backward_add(running, matrix, block):
        shaped = block.reshape(tok_rows, groups, group_size)
        return running + jnp.einsum(
            "gab,agc->bgc", matrix, shaped, preferred_element_type=jnp.float32
        ).reshape(tok_rows, channels)

    def window_add(buffer, grad_block, value_block, offset):
        left_side = grad_block.reshape(tok_rows, groups, group_size)
        right_side = value_block.reshape(tok_rows, groups, group_size)
        paired = jnp.einsum(
            "agc,bgc->gab", left_side, right_side, preferred_element_type=jnp.float32
        ).astype(jnp.bfloat16)
        window = diagonal_sums(paired)
        first_col = offset * tok_rows
        current = lax.dynamic_slice_in_dim(buffer, first_col, 2 * tok_rows, 1)
        return lax.dynamic_update_slice_in_dim(buffer, current + window, first_col, 1)

    def visit_block(carried, value_block, grad_block, offset, has_value, has_grad):
        convolved, grad_vals, buffer = carried
        bounded = jnp.minimum(offset, lag_blocks)
        matrix = toeplitz(padded_kernel, bounded, tok_rows)
        convolved = lax.cond(
            has_value, lambda: forward_add(convolved, matrix, value_block), lambda: convolved
        )
        grad_vals = lax.cond(
            has_grad, lambda: backward_add(grad_vals, matrix, grad_block), lambda: grad_vals
        )
        buffer = lax.cond(
            has_value, lambda: window_add(buffer, grad_mixed, value_block, bounded), lambda: buffer
        )
        return (convolved, grad_vals, buffer)

    initial = (
        jnp.zeros((tok_rows, channels), jnp.float32),
        jnp.zeros((tok_rows, channels), jnp.float32),
        jnp.zeros((groups, lag_count + 2 * tok_rows), jnp.float32),
    )
    value_shard = lax.all_gather(conv_input, "ctx", axis=1, tiled=True)
    grad_shard = lax.all_gather(grad_mixed[None], "ctx", axis=1, tiled=True)
    pieces = value_shard.shape[1] // tok_rows

    def per_block(position, carried_now):
        value_block = lax.dynamic_slice_in_dim(value_shard[0], position * tok_rows, tok_rows, 0)
        grad_block = lax.dynamic_slice_in_dim(grad_shard[0], position * tok_rows, tok_rows, 0)
        distance = jnp.abs(own_block - position)
        near = distance <= lag_blocks
        return visit_block(
            carried_now,
            value_block,
            grad_block,
            distance,
            (position <= own_block) & near,
            (position >= own_block) & near,
        )

    carried = lax.fori_loop(0, pieces, per_block, initial)
    convolved, grad_vals, buffer = carried
    output = (gate_rows.astype(jnp.float32) * convolved).astype(jnp.bfloat16)[None]
    grad_gate = (grad_rows.astype(jnp.float32) * convolved).astype(jnp.bfloat16)[None]
    grad_conv = grad_vals.astype(jnp.bfloat16)[None]
    partial_value = buffer[:, tok_rows - 1 : tok_rows - 1 + lag_count]
    summed = lax.psum_scatter(partial_value, ("dp", "ctx"), scatter_dimension=1, tiled=True)
    grad_kernel = summed / math.sqrt(lax.axis_size("dp") * tok_rows * blocks)
    return (output, grad_gate, grad_conv, grad_kernel)


TILE = 128
F32, BF16 = jnp.float32, jnp.bfloat16
MESH = pl.DeviceIdType.MESH


def dot(left, right):
    return jnp.dot(left, right, preferred_element_type=F32)


def dot_lanes(left, right):
    return lax.dot_general(left, right, (((1,), (1,)), ((), ())), preferred_element_type=F32)


def iota(shape, dim):
    return lax.broadcasted_iota(jnp.int32, shape, dim)


def fused_kernel(
    peers, scale,
    gate_ref, conv_ref, grad_ref, taps_ref,
    out_ref, ggate_ref, gconv_ref, gkern_ref,
    mixed, flipped, flipped_x, landed, other_x, other_g, zx, zg, rev_taps, mats, part, packed, arrived,
    block_send, block_recv, sum_send, sum_recv,
):
    rows, channels = conv_ref.shape
    groups = taps_ref.shape[0]
    size = channels // groups
    per_tile = TILE // size
    tiles = channels // TILE
    half = tiles // 2
    dp, ctx = lax.axis_index("dp"), lax.axis_index("ctx")
    me = dp * 2 + ctx
    share = gkern_ref.shape[1]

    def place(index):
        return {"dp": index // 2, "ctx": lax.rem(index, 2)}

    barrier = pltpu.get_barrier_semaphore()
    for step in range(1, peers):
        pl.semaphore_signal(barrier, inc=1, device_id=place(lax.rem(me + step, peers)), device_id_type=MESH)

    mixed[...] = (gate_ref[...].astype(F32) * grad_ref[...].astype(F32)).astype(BF16)
    row, col = iota((rows, rows), 0), iota((rows, rows), 1)
    lower = row >= col
    upper = row + col >= rows - 1
    backwards = jnp.where(row + col == rows - 1, 1.0, 0.0).astype(BF16)
    wrapped = jnp.where(lax.rem(row + col, rows) == 0, 1.0, 0.0).astype(BF16)
    rev_taps[0] = dot(taps_ref[:, :rows], wrapped)
    rev_taps[1] = dot(taps_ref[:, rows:], wrapped)

    pl.semaphore_wait(barrier, peers - 1)
    partner = {"ctx": 1 - ctx}

    def exchange(source):
        return pltpu.make_async_remote_copy(
            src_ref=source, dst_ref=landed, send_sem=block_send, recv_sem=block_recv,
            device_id=partner, device_id_type=MESH,
        )

    @pl.when(ctx == 0)
    def _():
        exchange(conv_ref).start()

    @pl.when(ctx == 1)
    def _():
        exchange(mixed).start()

    lane = iota((1, TILE), 1)
    masks = [((lane // size) == q).astype(F32).astype(BF16) for q in range(per_tile)]

    def lanes(tile):
        return pl.ds(pl.multiple_of(tile * TILE, TILE), TILE)

    def build(tile, _):
        for q in range(per_tile):
            group = pl.ds(tile * per_tile + q, 1)
            near, far = [
                pltpu.roll(jnp.broadcast_to(rev_taps[h, group, :], (rows, rows)), 0, 1, stride=1, stride_axis=0)
                for h in range(2)
            ]
            mats[tile, :, q * 2 * rows : q * 2 * rows + rows] = jnp.where(lower, near, 0.0).astype(BF16)
            mats[tile, :, q * 2 * rows + rows : (q + 1) * 2 * rows] = jnp.where(lower, far, near).astype(BF16)
        return 0

    def diagonals(matrix):
        turned = pltpu.roll(matrix, 0, 1, stride=1, stride_axis=0)
        return jnp.sum(turned, axis=0, keepdims=True)

    def masked(block):
        return jnp.concatenate([block * m for m in masks], axis=0)

    def pairs(tile):
        return dot_lanes(masked(flipped_x[:, lanes(tile)]), mixed[:, lanes(tile)])

    def near_only(step, _):
        tile = (1 - ctx) * half + step
        found = pairs(tile)
        for q in range(per_tile):
            group = pl.ds(tile * per_tile + q, 1)
            part[0, group, :] = diagonals(jnp.where(upper, found[q * rows : (q + 1) * rows], 0.0))
            part[1, group, :] = jnp.zeros((1, rows), F32)
        return 0

    def near_and_far(step, _):
        tile = ctx * half + step
        found = pairs(tile)
        across = dot_lanes(masked(other_x[:, lanes(tile)]), other_g[:, lanes(tile)])
        for q in range(per_tile):
            group = pl.ds(tile * per_tile + q, 1)
            inner, outer = found[q * rows : (q + 1) * rows], across[q * rows : (q + 1) * rows]
            part[0, group, :] = diagonals(jnp.where(upper, inner, outer))
            part[1, group, :] = diagonals(jnp.where(upper, outer, 0.0))
        return 0

    flipped_x[...] = dot(backwards, conv_ref[...]).astype(BF16)
    flipped[...] = dot(backwards, mixed[...]).astype(BF16)
    lax.fori_loop(0, tiles, build, 0)
    lax.fori_loop(0, half, near_only, 0)

    exchange(conv_ref).wait_recv()
    block = landed[...]
    turned_block = dot(backwards, block).astype(BF16)
    first = ctx == 0
    other_x[...] = jnp.where(first, flipped_x[...], turned_block)
    other_g[...] = jnp.where(first, block, mixed[...])
    lax.fori_loop(0, half, near_and_far, 0)

    for peer in range(peers):
        h, e = peer // (rows // share), peer % (rows // share)
        tile8 = jnp.zeros((8, TILE), F32)
        for j in range(groups // 8):
            value = part[h, 8 * j : 8 * j + 8, :]
            shift = (share * (j - e) + 1) % TILE
            if shift:
                value = pltpu.roll(value, shift, 1)
            tile8 = jnp.where(lane // share == j, value, tile8)
        packed[peer] = tile8

    def send_sum(step):
        peer = lax.rem(me + step, peers)
        return pltpu.make_async_remote_copy(
            src_ref=packed.at[peer], dst_ref=arrived.at[step],
            send_sem=sum_send.at[step], recv_sem=sum_recv.at[step],
            device_id=place(peer), device_id_type=MESH,
        )

    copies = [send_sum(step) for step in range(1, peers)]
    for copy in copies:
        copy.start()

    zx[...] = jnp.where(first, jnp.zeros_like(block), block)
    zg[...] = jnp.where(first, turned_block, jnp.zeros_like(block))

    def convolve(tile, _):
        at = lanes(tile)
        total = jnp.zeros((rows, 2 * TILE), F32)
        stacked = jnp.concatenate(
            [
                jnp.concatenate([conv_ref[:, at], flipped[:, at]], axis=1),
                jnp.concatenate([zx[:, at], zg[:, at]], axis=1),
            ],
            axis=0,
        )
        wide = jnp.concatenate([stacked * jnp.concatenate([m, m], axis=1) for m in masks], axis=0)
        total = dot(mats[tile], wide)
        convolved = total[:, :TILE]
        out_ref[:, at] = (gate_ref[:, at].astype(F32) * convolved).astype(BF16)
        ggate_ref[:, at] = (grad_ref[:, at].astype(F32) * convolved).astype(BF16)
        gconv_ref[:, at] = dot(backwards, total[:, TILE:].astype(BF16)).astype(BF16)
        return 0

    lax.fori_loop(0, tiles, convolve, 0)

    exchange(conv_ref).wait_send()
    summed = packed[me]
    for step, copy in zip(range(1, peers), copies):
        copy.wait()
        summed = summed + arrived[step]
    summed = summed * scale
    for j in range(groups // 8):
        value = summed if j == 0 else pltpu.roll(summed, TILE - share * j, 1)
        gkern_ref[8 * j : 8 * j + 8, :] = value[:, :share]


def fused_body(gate_input, conv_input, grad_output, kernel):
    _, rows, channels = conv_input.shape
    groups, lag_count = kernel.shape
    tiles = channels // TILE
    peers = lax.axis_size("dp") * lax.axis_size("ctx")
    scale = 1.0 / math.sqrt(lax.axis_size("dp") * rows * lax.axis_size("ctx"))
    block = jax.ShapeDtypeStruct((rows, channels), BF16)
    vmem = pl.BlockSpec(memory_space=pltpu.VMEM)
    results = pl.pallas_call(
        functools.partial(fused_kernel, peers, scale),
        out_shape=[block, block, block, jax.ShapeDtypeStruct((groups, lag_count // peers), F32)],
        in_specs=[vmem] * 4,
        out_specs=[vmem] * 4,
        scratch_shapes=[pltpu.VMEM((rows, channels), BF16)] * 8
        + [
            pltpu.VMEM((2, groups, rows), F32),
            pltpu.VMEM((tiles, rows, (groups // tiles) * 2 * rows), BF16),
            pltpu.VMEM((2, groups, rows), F32),
            pltpu.VMEM((peers, 8, TILE), F32),
            pltpu.VMEM((peers, 8, TILE), F32),
            pltpu.SemaphoreType.DMA,
            pltpu.SemaphoreType.DMA,
            pltpu.SemaphoreType.DMA((peers,)),
            pltpu.SemaphoreType.DMA((peers,)),
        ],
        compiler_params=pltpu.CompilerParams(
            collective_id=0, has_side_effects=True, vmem_limit_bytes=48 * 1024 * 1024
        ),
        cost_estimate=pl.CostEstimate(
            flops=20 * rows * rows * channels, bytes_accessed=12 * rows * channels, transcendentals=0
        ),
    )(gate_input[0], conv_input[0], grad_output[0], kernel)
    return (results[0][None], results[1][None], results[2][None], results[3])


def body(gate_input, conv_input, grad_output, kernel):
    _, rows, channels = conv_input.shape
    groups, lag_count = kernel.shape
    peers = lax.axis_size("dp") * lax.axis_size("ctx")
    fits = (
        lax.axis_size("ctx") == 2
        and rows == TILE
        and lag_count == 2 * rows
        and channels % (2 * TILE) == 0
        and TILE % (channels // groups) == 0
        and lag_count % peers == 0
        and rows % (lag_count // peers) == 0
        and groups * (lag_count // peers) == 8 * TILE
    )
    if fits:
        return fused_body(gate_input, conv_input, grad_output, kernel)
    return general_body(gate_input, conv_input, grad_output, kernel)


def solution(mesh):
    return jax.shard_map(
        body,
        mesh=mesh,
        in_specs=(P("dp", "ctx", "ch"), P("dp", "ctx", "ch"), P("dp", "ctx", "ch"), P("ch", None)),
        out_specs=(
            P("dp", "ctx", "ch"),
            P("dp", "ctx", "ch"),
            P("dp", "ctx", "ch"),
            P("ch", ("dp", "ctx")),
        ),
        check_vma=False,
    )
```

```python
import functools
import math

import jax
import jax.numpy as jnp
from jax import lax
from jax.experimental import pallas as pl
from jax.experimental.pallas import tpu as pltpu
from jax.sharding import PartitionSpec as P


def toeplitz(padded_kernel, offset, tok_rows):
    groups = padded_kernel.shape[0]
    segment = lax.dynamic_slice_in_dim(padded_kernel, offset * tok_rows + 1, 2 * tok_rows, 1)
    reverse = segment[:, ::-1]
    rolled = jnp.concatenate([reverse[:, tok_rows:], reverse[:, :tok_rows]], axis=1)
    tiled = jnp.tile(rolled, (1, tok_rows))[:, : tok_rows * (2 * tok_rows - 1)]
    return tiled.reshape(groups, tok_rows, 2 * tok_rows - 1)[:, :, :tok_rows]


def diagonal_sums(matrix):
    groups = matrix.shape[0]
    extent = matrix.shape[1]
    flipped = matrix[:, :, ::-1]
    padded = jnp.pad(flipped, ((0, 0), (0, 0), (0, extent)))
    flattened = padded.reshape(groups, 2 * extent * extent)[:, : extent * (2 * extent - 1)]
    totals = jnp.sum(flattened.reshape(groups, extent, 2 * extent - 1), axis=1, dtype=jnp.float32)
    return jnp.pad(totals, ((0, 0), (0, 1)))


def general_body(gate_input, conv_input, grad_output, kernel):
    tok_rows = gate_input.shape[1]
    channels = gate_input.shape[2]
    groups = kernel.shape[0]
    group_size = channels // groups
    lag_count = kernel.shape[1]
    lag_blocks = lag_count // tok_rows
    padded_kernel = jnp.pad(kernel, ((0, 0), (tok_rows, 2 * tok_rows)))
    blocks = lax.axis_size("ctx")
    own_block = lax.axis_index("ctx")
    gate_rows = gate_input[0]
    grad_rows = grad_output[0]
    grad_mixed = (gate_rows.astype(jnp.float32) * grad_rows.astype(jnp.float32)).astype(
        jnp.bfloat16
    )

    def forward_add(running, matrix, block):
        shaped = block.reshape(tok_rows, groups, group_size)
        return running + jnp.einsum(
            "gab,bgc->agc", matrix, shaped, preferred_element_type=jnp.float32
        ).reshape(tok_rows, channels)

    def backward_add(running, matrix, block):
        shaped = block.reshape(tok_rows, groups, group_size)
        return running + jnp.einsum(
            "gab,agc->bgc", matrix, shaped, preferred_element_type=jnp.float32
        ).reshape(tok_rows, channels)

    def window_add(buffer, grad_block, value_block, offset):
        left_side = grad_block.reshape(tok_rows, groups, group_size)
        right_side = value_block.reshape(tok_rows, groups, group_size)
        paired = jnp.einsum(
            "agc,bgc->gab", left_side, right_side, preferred_element_type=jnp.float32
        ).astype(jnp.bfloat16)
        window = diagonal_sums(paired)
        first_col = offset * tok_rows
        current = lax.dynamic_slice_in_dim(buffer, first_col, 2 * tok_rows, 1)
        return lax.dynamic_update_slice_in_dim(buffer, current + window, first_col, 1)

    def visit_block(carried, value_block, grad_block, offset, has_value, has_grad):
        convolved, grad_vals, buffer = carried
        bounded = jnp.minimum(offset, lag_blocks)
        matrix = toeplitz(padded_kernel, bounded, tok_rows)
        convolved = lax.cond(
            has_value, lambda: forward_add(convolved, matrix, value_block), lambda: convolved
        )
        grad_vals = lax.cond(
            has_grad, lambda: backward_add(grad_vals, matrix, grad_block), lambda: grad_vals
        )
        buffer = lax.cond(
            has_value, lambda: window_add(buffer, grad_mixed, value_block, bounded), lambda: buffer
        )
        return (convolved, grad_vals, buffer)

    initial = (
        jnp.zeros((tok_rows, channels), jnp.float32),
        jnp.zeros((tok_rows, channels), jnp.float32),
        jnp.zeros((groups, lag_count + 2 * tok_rows), jnp.float32),
    )
    value_shard = lax.all_gather(conv_input, "ctx", axis=1, tiled=True)
    grad_shard = lax.all_gather(grad_mixed[None], "ctx", axis=1, tiled=True)
    pieces = value_shard.shape[1] // tok_rows

    def per_block(position, carried_now):
        value_block = lax.dynamic_slice_in_dim(value_shard[0], position * tok_rows, tok_rows, 0)
        grad_block = lax.dynamic_slice_in_dim(grad_shard[0], position * tok_rows, tok_rows, 0)
        distance = jnp.abs(own_block - position)
        near = distance <= lag_blocks
        return visit_block(
            carried_now,
            value_block,
            grad_block,
            distance,
            (position <= own_block) & near,
            (position >= own_block) & near,
        )

    carried = lax.fori_loop(0, pieces, per_block, initial)
    convolved, grad_vals, buffer = carried
    output = (gate_rows.astype(jnp.float32) * convolved).astype(jnp.bfloat16)[None]
    grad_gate = (grad_rows.astype(jnp.float32) * convolved).astype(jnp.bfloat16)[None]
    grad_conv = grad_vals.astype(jnp.bfloat16)[None]
    partial_value = buffer[:, tok_rows - 1 : tok_rows - 1 + lag_count]
    summed = lax.psum_scatter(partial_value, ("dp", "ctx"), scatter_dimension=1, tiled=True)
    grad_kernel = summed / math.sqrt(lax.axis_size("dp") * tok_rows * blocks)
    return (output, grad_gate, grad_conv, grad_kernel)


TILE = 128
VMEM_BYTES = 60 * 1024 * 1024
F32, BF16 = jnp.float32, jnp.bfloat16
MESH = pl.DeviceIdType.MESH


def dot(left, right):
    return jnp.dot(left, right, preferred_element_type=F32)


def dot_lanes(left, right):
    return lax.dot_general(left, right, (((1,), (1,)), ((), ())), preferred_element_type=F32)


def iota(shape, dim):
    return lax.broadcasted_iota(jnp.int32, shape, dim)


def fused_kernel(
    peers, scale,
    gate_hbm, conv_hbm, grad_hbm, taps_hbm,
    out_hbm, ggate_hbm, gconv_hbm, gkern_ref,
    out_ref, ggate_ref, gconv_ref, gate_ref, conv_ref, grad_ref, taps_ref, mixed, flipped, flipped_x, landed, other_x, other_g, zx, zg, turned_out, rev_taps, mats, part, packed, arrived,
    load_sem, save_sem, block_send, block_recv, sum_send, sum_recv,
):
    rows, channels = conv_ref.shape
    groups = taps_ref.shape[0]
    size = channels // groups
    per_tile = TILE // size
    tiles = channels // TILE
    half = tiles // 2
    dp, ctx = lax.axis_index("dp"), lax.axis_index("ctx")
    me = dp * 2 + ctx
    share = gkern_ref.shape[1]

    def place(index):
        return {"dp": index // 2, "ctx": lax.rem(index, 2)}

    loads = [
        pltpu.make_async_copy(source, target, load_sem.at[i])
        for i, (source, target) in enumerate(
            [(taps_hbm, taps_ref), (gate_hbm, gate_ref), (grad_hbm, grad_ref), (conv_hbm, conv_ref)]
        )
    ]
    for load in loads:
        load.start()

    barrier = pltpu.get_barrier_semaphore()
    for step in range(1, peers):
        pl.semaphore_signal(barrier, inc=1, device_id=place(lax.rem(me + step, peers)), device_id_type=MESH)

    row, col = iota((rows, rows), 0), iota((rows, rows), 1)
    lower = row >= col
    upper = row + col >= rows - 1
    backwards = jnp.where(row + col == rows - 1, 1.0, 0.0).astype(BF16)
    wrapped = jnp.where(lax.rem(row + col, rows) == 0, 1.0, 0.0).astype(BF16)
    loads[0].wait()
    rev_taps[0] = dot(taps_ref[:, :rows], wrapped)
    rev_taps[1] = dot(taps_ref[:, rows:], wrapped)

    lane = iota((1, TILE), 1)
    masks = [((lane // size) == q).astype(F32).astype(BF16) for q in range(per_tile)]

    def lanes(tile):
        start = tile * TILE
        return pl.ds(start if isinstance(tile, int) else pl.multiple_of(start, TILE), TILE)

    def build(tile):
        for q in range(per_tile):
            group = pl.ds(tile * per_tile + q, 1)
            near, far = [
                pltpu.roll(jnp.broadcast_to(rev_taps[h, group, :], (rows, rows)), 0, 1, stride=1, stride_axis=0)
                for h in range(2)
            ]
            mats[tile, :, q * 2 * rows : q * 2 * rows + rows] = jnp.where(lower, near, 0.0).astype(BF16)
            mats[tile, :, q * 2 * rows + rows : (q + 1) * 2 * rows] = jnp.where(lower, far, near).astype(BF16)

    def diagonals(matrix):
        turned = pltpu.roll(matrix, 0, 1, stride=1, stride_axis=0)
        return jnp.sum(turned, axis=0, keepdims=True)

    def masked(block):
        return jnp.concatenate([block * m for m in masks], axis=0)

    def pairs(tile):
        return dot_lanes(masked(flipped_x[:, lanes(tile)]), mixed[:, lanes(tile)])

    def near_only(step):
        tile = (1 - ctx) * half + step
        found = pairs(tile)
        for q in range(per_tile):
            group = pl.ds(tile * per_tile + q, 1)
            part[0, group, :] = diagonals(jnp.where(upper, found[q * rows : (q + 1) * rows], 0.0))
            part[1, group, :] = jnp.zeros((1, rows), F32)

    def near_and_far(step):
        tile = ctx * half + step
        found = pairs(tile)
        across = dot_lanes(masked(other_x[:, lanes(tile)]), other_g[:, lanes(tile)])
        for q in range(per_tile):
            group = pl.ds(tile * per_tile + q, 1)
            inner, outer = found[q * rows : (q + 1) * rows], across[q * rows : (q + 1) * rows]
            part[0, group, :] = diagonals(jnp.where(upper, inner, outer))
            part[1, group, :] = diagonals(jnp.where(upper, outer, 0.0))

    for tile in range(half):
        build(tile)
    for load in loads[1:]:
        load.wait()
    mixed[...] = (gate_ref[...].astype(F32) * grad_ref[...].astype(F32)).astype(BF16)

    pl.semaphore_wait(barrier, peers - 1)
    partner = {"ctx": 1 - ctx}

    def exchange(source):
        return pltpu.make_async_remote_copy(
            src_ref=source, dst_ref=landed, send_sem=block_send, recv_sem=block_recv,
            device_id=partner, device_id_type=MESH,
        )

    @pl.when(ctx == 0)
    def _():
        exchange(conv_ref).start()

    @pl.when(ctx == 1)
    def _():
        exchange(mixed).start()

    for tile in range(half, tiles):
        build(tile)
    flipped_x[...] = dot(backwards, conv_ref[...]).astype(BF16)
    flipped[...] = dot(backwards, mixed[...]).astype(BF16)
    for step in range(half):
        near_only(step)

    exchange(conv_ref).wait_recv()
    block = landed[...]
    turned_block = dot(backwards, block).astype(BF16)
    first = ctx == 0
    other_x[...] = jnp.where(first, flipped_x[...], turned_block)
    other_g[...] = jnp.where(first, block, mixed[...])
    for step in range(half):
        near_and_far(step)

    for peer in range(peers):
        h, e = peer // (rows // share), peer % (rows // share)
        tile8 = jnp.zeros((8, TILE), F32)
        for j in range(groups // 8):
            value = part[h, 8 * j : 8 * j + 8, :]
            shift = (share * (j - e) + 1) % TILE
            if shift:
                value = pltpu.roll(value, shift, 1)
            tile8 = jnp.where(lane // share == j, value, tile8)
        packed[peer] = tile8

    def send_sum(step):
        peer = lax.rem(me + step, peers)
        return pltpu.make_async_remote_copy(
            src_ref=packed.at[peer], dst_ref=arrived.at[step],
            send_sem=sum_send.at[step], recv_sem=sum_recv.at[step],
            device_id=place(peer), device_id_type=MESH,
        )

    copies = [send_sum(step) for step in range(1, peers)]
    for copy in copies:
        copy.start()

    zx[...] = jnp.where(first, jnp.zeros_like(block), block)
    zg[...] = jnp.where(first, turned_block, jnp.zeros_like(block))

    def convolve(tile):
        at = lanes(tile)
        stacked = jnp.concatenate(
            [
                jnp.concatenate([conv_ref[:, at], flipped[:, at]], axis=1),
                jnp.concatenate([zx[:, at], zg[:, at]], axis=1),
            ],
            axis=0,
        )
        wide = jnp.concatenate([stacked * jnp.concatenate([m, m], axis=1) for m in masks], axis=0)
        total = dot(mats[tile], wide)
        convolved = total[:, :TILE]
        out_ref[:, at] = (gate_ref[:, at].astype(F32) * convolved).astype(BF16)
        ggate_ref[:, at] = (grad_ref[:, at].astype(F32) * convolved).astype(BF16)
        turned_out[:, at] = total[:, TILE:].astype(BF16)

    saves = []
    for part_index in range(2):
        for tile in range(part_index * half, (part_index + 1) * half):
            convolve(tile)
        at = slice(part_index * half * TILE, (part_index + 1) * half * TILE)
        gconv_ref[:, at] = dot(backwards, turned_out[:, at]).astype(BF16)
        for i, (source, target) in enumerate([(out_ref, out_hbm), (ggate_ref, ggate_hbm), (gconv_ref, gconv_hbm)]):
            saves.append(pltpu.make_async_copy(source.at[:, at], target.at[:, at], save_sem.at[part_index, i]))
            saves[-1].start()

    exchange(conv_ref).wait_send()
    summed = packed[me]
    for step, copy in zip(range(1, peers), copies):
        copy.wait()
        summed = summed + arrived[step]
    summed = summed * scale
    for j in range(groups // 8):
        value = summed if j == 0 else pltpu.roll(summed, TILE - share * j, 1)
        gkern_ref[8 * j : 8 * j + 8, :] = value[:, :share]
    for save in saves:
        save.wait()


def store_kernel(*refs):
    sems = refs[-1]
    copies = [pltpu.make_async_copy(refs[i], refs[4 + i], sems.at[i]) for i in range(4)]
    for copy in copies:
        copy.start()
    for copy in copies:
        copy.wait()


def fused_body(gate_input, conv_input, grad_output, kernel):
    _, rows, channels = conv_input.shape
    groups, lag_count = kernel.shape
    tiles = channels // TILE
    peers = lax.axis_size("dp") * lax.axis_size("ctx")
    scale = 1.0 / math.sqrt(lax.axis_size("dp") * rows * lax.axis_size("ctx"))
    block = jax.ShapeDtypeStruct((rows, channels), BF16)
    vmem = pl.BlockSpec(memory_space=pltpu.VMEM)
    hbm = pl.BlockSpec(memory_space=pltpu.HBM)
    results = pl.pallas_call(
        functools.partial(fused_kernel, peers, scale),
        out_shape=[block, block, block, jax.ShapeDtypeStruct((groups, lag_count // peers), F32)],
        in_specs=[hbm] * 4,
        out_specs=[hbm] * 3 + [vmem],
        scratch_shapes=[pltpu.VMEM((rows, channels), BF16)] * 6
        + [pltpu.VMEM((groups, lag_count), BF16)]
        + [pltpu.VMEM((rows, channels), BF16)] * 9
        + [
            pltpu.VMEM((2, groups, rows), F32),
            pltpu.VMEM((tiles, rows, (groups // tiles) * 2 * rows), BF16),
            pltpu.VMEM((2, groups, rows), F32),
            pltpu.VMEM((peers, 8, TILE), F32),
            pltpu.VMEM((peers, 8, TILE), F32),
            pltpu.SemaphoreType.DMA((4,)),
            pltpu.SemaphoreType.DMA((2, 3)),
            pltpu.SemaphoreType.DMA,
            pltpu.SemaphoreType.DMA,
            pltpu.SemaphoreType.DMA((peers,)),
            pltpu.SemaphoreType.DMA((peers,)),
        ],
        compiler_params=pltpu.CompilerParams(
            collective_id=0, has_side_effects=True, vmem_limit_bytes=VMEM_BYTES
        ),
        cost_estimate=pl.CostEstimate(
            flops=20 * rows * rows * channels, bytes_accessed=12 * rows * channels, transcendentals=0
        ),
    )(gate_input[0], conv_input[0], grad_output[0], kernel)
    results = pl.pallas_call(
        store_kernel,
        out_shape=[block, block, block, jax.ShapeDtypeStruct((groups, lag_count // peers), F32)],
        in_specs=[hbm] * 4,
        out_specs=[hbm] * 4,
        scratch_shapes=[pltpu.SemaphoreType.DMA((4,))],
        compiler_params=pltpu.CompilerParams(vmem_limit_bytes=VMEM_BYTES),
    )(*results)
    return (results[0][None], results[1][None], results[2][None], results[3])


def body(gate_input, conv_input, grad_output, kernel):
    _, rows, channels = conv_input.shape
    groups, lag_count = kernel.shape
    peers = lax.axis_size("dp") * lax.axis_size("ctx")
    fits = (
        lax.axis_size("ctx") == 2
        and rows == TILE
        and lag_count == 2 * rows
        and channels % (2 * TILE) == 0
        and TILE % (channels // groups) == 0
        and lag_count % peers == 0
        and rows % (lag_count // peers) == 0
        and groups * (lag_count // peers) == 8 * TILE
    )
    if fits:
        return fused_body(gate_input, conv_input, grad_output, kernel)
    return general_body(gate_input, conv_input, grad_output, kernel)


def solution(mesh):
    return jax.shard_map(
        body,
        mesh=mesh,
        in_specs=(P("dp", "ctx", "ch"), P("dp", "ctx", "ch"), P("dp", "ctx", "ch"), P("ch", None)),
        out_specs=(
            P("dp", "ctx", "ch"),
            P("dp", "ctx", "ch"),
            P("dp", "ctx", "ch"),
            P("ch", ("dp", "ctx")),
        ),
        check_vma=False,
    )
```

```python
import functools
import math

import jax
import jax.numpy as jnp
from jax import lax
from jax.experimental import pallas as pl
from jax.experimental.pallas import tpu as pltpu
from jax.sharding import PartitionSpec as P


def toeplitz(padded_kernel, offset, tok_rows):
    groups = padded_kernel.shape[0]
    segment = lax.dynamic_slice_in_dim(padded_kernel, offset * tok_rows + 1, 2 * tok_rows, 1)
    reverse = segment[:, ::-1]
    rolled = jnp.concatenate([reverse[:, tok_rows:], reverse[:, :tok_rows]], axis=1)
    tiled = jnp.tile(rolled, (1, tok_rows))[:, : tok_rows * (2 * tok_rows - 1)]
    return tiled.reshape(groups, tok_rows, 2 * tok_rows - 1)[:, :, :tok_rows]


def diagonal_sums(matrix):
    groups = matrix.shape[0]
    extent = matrix.shape[1]
    flipped = matrix[:, :, ::-1]
    padded = jnp.pad(flipped, ((0, 0), (0, 0), (0, extent)))
    flattened = padded.reshape(groups, 2 * extent * extent)[:, : extent * (2 * extent - 1)]
    totals = jnp.sum(flattened.reshape(groups, extent, 2 * extent - 1), axis=1, dtype=jnp.float32)
    return jnp.pad(totals, ((0, 0), (0, 1)))


def general_body(gate_input, conv_input, grad_output, kernel):
    tok_rows = gate_input.shape[1]
    channels = gate_input.shape[2]
    groups = kernel.shape[0]
    group_size = channels // groups
    lag_count = kernel.shape[1]
    lag_blocks = lag_count // tok_rows
    padded_kernel = jnp.pad(kernel, ((0, 0), (tok_rows, 2 * tok_rows)))
    blocks = lax.axis_size("ctx")
    own_block = lax.axis_index("ctx")
    gate_rows = gate_input[0]
    grad_rows = grad_output[0]
    grad_mixed = (gate_rows.astype(jnp.float32) * grad_rows.astype(jnp.float32)).astype(
        jnp.bfloat16
    )

    def forward_add(running, matrix, block):
        shaped = block.reshape(tok_rows, groups, group_size)
        return running + jnp.einsum(
            "gab,bgc->agc", matrix, shaped, preferred_element_type=jnp.float32
        ).reshape(tok_rows, channels)

    def backward_add(running, matrix, block):
        shaped = block.reshape(tok_rows, groups, group_size)
        return running + jnp.einsum(
            "gab,agc->bgc", matrix, shaped, preferred_element_type=jnp.float32
        ).reshape(tok_rows, channels)

    def window_add(buffer, grad_block, value_block, offset):
        left_side = grad_block.reshape(tok_rows, groups, group_size)
        right_side = value_block.reshape(tok_rows, groups, group_size)
        paired = jnp.einsum(
            "agc,bgc->gab", left_side, right_side, preferred_element_type=jnp.float32
        ).astype(jnp.bfloat16)
        window = diagonal_sums(paired)
        first_col = offset * tok_rows
        current = lax.dynamic_slice_in_dim(buffer, first_col, 2 * tok_rows, 1)
        return lax.dynamic_update_slice_in_dim(buffer, current + window, first_col, 1)

    def visit_block(carried, value_block, grad_block, offset, has_value, has_grad):
        convolved, grad_vals, buffer = carried
        bounded = jnp.minimum(offset, lag_blocks)
        matrix = toeplitz(padded_kernel, bounded, tok_rows)
        convolved = lax.cond(
            has_value, lambda: forward_add(convolved, matrix, value_block), lambda: convolved
        )
        grad_vals = lax.cond(
            has_grad, lambda: backward_add(grad_vals, matrix, grad_block), lambda: grad_vals
        )
        buffer = lax.cond(
            has_value, lambda: window_add(buffer, grad_mixed, value_block, bounded), lambda: buffer
        )
        return (convolved, grad_vals, buffer)

    initial = (
        jnp.zeros((tok_rows, channels), jnp.float32),
        jnp.zeros((tok_rows, channels), jnp.float32),
        jnp.zeros((groups, lag_count + 2 * tok_rows), jnp.float32),
    )
    value_shard = lax.all_gather(conv_input, "ctx", axis=1, tiled=True)
    grad_shard = lax.all_gather(grad_mixed[None], "ctx", axis=1, tiled=True)
    pieces = value_shard.shape[1] // tok_rows

    def per_block(position, carried_now):
        value_block = lax.dynamic_slice_in_dim(value_shard[0], position * tok_rows, tok_rows, 0)
        grad_block = lax.dynamic_slice_in_dim(grad_shard[0], position * tok_rows, tok_rows, 0)
        distance = jnp.abs(own_block - position)
        near = distance <= lag_blocks
        return visit_block(
            carried_now,
            value_block,
            grad_block,
            distance,
            (position <= own_block) & near,
            (position >= own_block) & near,
        )

    carried = lax.fori_loop(0, pieces, per_block, initial)
    convolved, grad_vals, buffer = carried
    output = (gate_rows.astype(jnp.float32) * convolved).astype(jnp.bfloat16)[None]
    grad_gate = (grad_rows.astype(jnp.float32) * convolved).astype(jnp.bfloat16)[None]
    grad_conv = grad_vals.astype(jnp.bfloat16)[None]
    partial_value = buffer[:, tok_rows - 1 : tok_rows - 1 + lag_count]
    summed = lax.psum_scatter(partial_value, ("dp", "ctx"), scatter_dimension=1, tiled=True)
    grad_kernel = summed / math.sqrt(lax.axis_size("dp") * tok_rows * blocks)
    return (output, grad_gate, grad_conv, grad_kernel)


TILE = 128
VMEM_BYTES = 53 * 1024 * 1024
F32, BF16 = jnp.float32, jnp.bfloat16
MESH = pl.DeviceIdType.MESH


def dot(left, right):
    return jnp.dot(left, right, preferred_element_type=F32)


def dot_lanes(left, right):
    return lax.dot_general(left, right, (((1,), (1,)), ((), ())), preferred_element_type=F32)


def iota(shape, dim):
    return lax.broadcasted_iota(jnp.int32, shape, dim)


def fused_kernel(
    peers, scale,
    gate_hbm, conv_hbm, grad_hbm, taps_hbm,
    out_ref, ggate_ref, gconv_ref, gkern_ref,
    gate_ref, conv_ref, grad_ref, taps_ref, mixed, flipped, flipped_x, landed, other_x, other_g, zx, zg, turned_out, rev_taps, mats, part, packed, arrived,
    load_sem, save_sem, block_send, block_recv, sum_send, sum_recv,
):
    rows, channels = conv_ref.shape
    groups = taps_ref.shape[0]
    size = channels // groups
    per_tile = TILE // size
    tiles = channels // TILE
    half = tiles // 2
    dp, ctx = lax.axis_index("dp"), lax.axis_index("ctx")
    me = dp * 2 + ctx
    share = gkern_ref.shape[1]

    def place(index):
        return {"dp": index // 2, "ctx": lax.rem(index, 2)}

    loads = [
        pltpu.make_async_copy(source, target, load_sem.at[i])
        for i, (source, target) in enumerate(
            [(taps_hbm, taps_ref), (gate_hbm, gate_ref), (grad_hbm, grad_ref), (conv_hbm, conv_ref)]
        )
    ]
    for load in loads:
        load.start()

    barrier = pltpu.get_barrier_semaphore()
    for step in range(1, peers):
        pl.semaphore_signal(barrier, inc=1, device_id=place(lax.rem(me + step, peers)), device_id_type=MESH)

    row, col = iota((rows, rows), 0), iota((rows, rows), 1)
    lower = row >= col
    upper = row + col >= rows - 1
    backwards = jnp.where(row + col == rows - 1, 1.0, 0.0).astype(BF16)
    wrapped = jnp.where(lax.rem(row + col, rows) == 0, 1.0, 0.0).astype(BF16)
    loads[0].wait()
    rev_taps[0] = dot(taps_ref[:, :rows], wrapped)
    rev_taps[1] = dot(taps_ref[:, rows:], wrapped)

    lane = iota((1, TILE), 1)
    masks = [((lane // size) == q).astype(F32).astype(BF16) for q in range(per_tile)]

    def lanes(tile):
        start = tile * TILE
        return pl.ds(start if isinstance(tile, int) else pl.multiple_of(start, TILE), TILE)

    def build(tile):
        for q in range(per_tile):
            group = pl.ds(tile * per_tile + q, 1)
            near, far = [
                pltpu.roll(jnp.broadcast_to(rev_taps[h, group, :], (rows, rows)), 0, 1, stride=1, stride_axis=0)
                for h in range(2)
            ]
            mats[tile, :, q * 2 * rows : q * 2 * rows + rows] = jnp.where(lower, near, 0.0).astype(BF16)
            mats[tile, :, q * 2 * rows + rows : (q + 1) * 2 * rows] = jnp.where(lower, far, near).astype(BF16)

    def diagonals(matrix):
        turned = pltpu.roll(matrix, 0, 1, stride=1, stride_axis=0)
        return jnp.sum(turned, axis=0, keepdims=True)

    def masked(block):
        return jnp.concatenate([block * m for m in masks], axis=0)

    def pairs(tile):
        return dot_lanes(masked(flipped_x[:, lanes(tile)]), mixed[:, lanes(tile)])

    def near_only(step):
        tile = (1 - ctx) * half + step
        found = pairs(tile)
        for q in range(per_tile):
            group = pl.ds(tile * per_tile + q, 1)
            part[0, group, :] = diagonals(jnp.where(upper, found[q * rows : (q + 1) * rows], 0.0))
            part[1, group, :] = jnp.zeros((1, rows), F32)

    def near_and_far(step):
        tile = ctx * half + step
        found = pairs(tile)
        across = dot_lanes(masked(other_x[:, lanes(tile)]), other_g[:, lanes(tile)])
        for q in range(per_tile):
            group = pl.ds(tile * per_tile + q, 1)
            inner, outer = found[q * rows : (q + 1) * rows], across[q * rows : (q + 1) * rows]
            part[0, group, :] = diagonals(jnp.where(upper, inner, outer))
            part[1, group, :] = diagonals(jnp.where(upper, outer, 0.0))

    for tile in range(half):
        build(tile)
    for load in loads[1:]:
        load.wait()
    mixed[...] = (gate_ref[...].astype(F32) * grad_ref[...].astype(F32)).astype(BF16)

    pl.semaphore_wait(barrier, peers - 1)
    partner = {"ctx": 1 - ctx}

    def exchange(source):
        return pltpu.make_async_remote_copy(
            src_ref=source, dst_ref=landed, send_sem=block_send, recv_sem=block_recv,
            device_id=partner, device_id_type=MESH,
        )

    @pl.when(ctx == 0)
    def _():
        exchange(conv_ref).start()

    @pl.when(ctx == 1)
    def _():
        exchange(mixed).start()

    for tile in range(half, tiles):
        build(tile)
    flipped_x[...] = dot(backwards, conv_ref[...]).astype(BF16)
    flipped[...] = dot(backwards, mixed[...]).astype(BF16)
    for step in range(half):
        near_only(step)

    exchange(conv_ref).wait_recv()
    block = landed[...]
    turned_block = dot(backwards, block).astype(BF16)
    first = ctx == 0
    other_x[...] = jnp.where(first, flipped_x[...], turned_block)
    other_g[...] = jnp.where(first, block, mixed[...])
    for step in range(half):
        near_and_far(step)

    for peer in range(peers):
        h, e = peer // (rows // share), peer % (rows // share)
        tile8 = jnp.zeros((8, TILE), F32)
        for j in range(groups // 8):
            value = part[h, 8 * j : 8 * j + 8, :]
            shift = (share * (j - e) + 1) % TILE
            if shift:
                value = pltpu.roll(value, shift, 1)
            tile8 = jnp.where(lane // share == j, value, tile8)
        packed[peer] = tile8

    def send_sum(step):
        peer = lax.rem(me + step, peers)
        return pltpu.make_async_remote_copy(
            src_ref=packed.at[peer], dst_ref=arrived.at[step],
            send_sem=sum_send.at[step], recv_sem=sum_recv.at[step],
            device_id=place(peer), device_id_type=MESH,
        )

    copies = [send_sum(step) for step in range(1, peers)]
    for copy in copies:
        copy.start()

    zx[...] = jnp.where(first, jnp.zeros_like(block), block)
    zg[...] = jnp.where(first, turned_block, jnp.zeros_like(block))

    def convolve(tile):
        at = lanes(tile)
        stacked = jnp.concatenate(
            [
                jnp.concatenate([conv_ref[:, at], flipped[:, at]], axis=1),
                jnp.concatenate([zx[:, at], zg[:, at]], axis=1),
            ],
            axis=0,
        )
        wide = jnp.concatenate([stacked * jnp.concatenate([m, m], axis=1) for m in masks], axis=0)
        total = dot(mats[tile], wide)
        convolved = total[:, :TILE]
        out_ref[:, at] = (gate_ref[:, at].astype(F32) * convolved).astype(BF16)
        ggate_ref[:, at] = (grad_ref[:, at].astype(F32) * convolved).astype(BF16)
        turned_out[:, at] = total[:, TILE:].astype(BF16)

    saves = []
    for part_index in range(2):
        for tile in range(part_index * half, (part_index + 1) * half):
            convolve(tile)
        at = slice(part_index * half * TILE, (part_index + 1) * half * TILE)
        gconv_ref[:, at] = dot(backwards, turned_out[:, at]).astype(BF16)

    exchange(conv_ref).wait_send()
    summed = packed[me]
    for step, copy in zip(range(1, peers), copies):
        copy.wait()
        summed = summed + arrived[step]
    summed = summed * scale
    for j in range(groups // 8):
        value = summed if j == 0 else pltpu.roll(summed, TILE - share * j, 1)
        gkern_ref[8 * j : 8 * j + 8, :] = value[:, :share]
    for save in saves:
        save.wait()


def store_kernel(*refs):
    sems = refs[-1]
    copies = [pltpu.make_async_copy(refs[i], refs[4 + i], sems.at[i]) for i in range(4)]
    for copy in copies:
        copy.start()
    for copy in copies:
        copy.wait()


def fused_body(gate_input, conv_input, grad_output, kernel):
    _, rows, channels = conv_input.shape
    groups, lag_count = kernel.shape
    tiles = channels // TILE
    peers = lax.axis_size("dp") * lax.axis_size("ctx")
    scale = 1.0 / math.sqrt(lax.axis_size("dp") * rows * lax.axis_size("ctx"))
    block = jax.ShapeDtypeStruct((rows, channels), BF16)
    vmem = pl.BlockSpec(memory_space=pltpu.VMEM)
    hbm = pl.BlockSpec(memory_space=pltpu.HBM)
    results = pl.pallas_call(
        functools.partial(fused_kernel, peers, scale),
        out_shape=[block, block, block, jax.ShapeDtypeStruct((groups, lag_count // peers), F32)],
        in_specs=[hbm] * 4,
        out_specs=[vmem] * 4,
        scratch_shapes=[pltpu.VMEM((rows, channels), BF16)] * 3
        + [pltpu.VMEM((groups, lag_count), BF16)]
        + [pltpu.VMEM((rows, channels), BF16)] * 9
        + [
            pltpu.VMEM((2, groups, rows), F32),
            pltpu.VMEM((tiles, rows, (groups // tiles) * 2 * rows), BF16),
            pltpu.VMEM((2, groups, rows), F32),
            pltpu.VMEM((peers, 8, TILE), F32),
            pltpu.VMEM((peers, 8, TILE), F32),
            pltpu.SemaphoreType.DMA((4,)),
            pltpu.SemaphoreType.DMA((2, 3)),
            pltpu.SemaphoreType.DMA,
            pltpu.SemaphoreType.DMA,
            pltpu.SemaphoreType.DMA((peers,)),
            pltpu.SemaphoreType.DMA((peers,)),
        ],
        compiler_params=pltpu.CompilerParams(
            collective_id=0, has_side_effects=True, vmem_limit_bytes=VMEM_BYTES
        ),
        cost_estimate=pl.CostEstimate(
            flops=20 * rows * rows * channels, bytes_accessed=12 * rows * channels, transcendentals=0
        ),
    )(gate_input[0], conv_input[0], grad_output[0], kernel)
    results = pl.pallas_call(
        store_kernel,
        out_shape=[block, block, block, jax.ShapeDtypeStruct((groups, lag_count // peers), F32)],
        in_specs=[vmem] * 4,
        out_specs=[hbm] * 4,
        scratch_shapes=[pltpu.SemaphoreType.DMA((4,))],
        compiler_params=pltpu.CompilerParams(vmem_limit_bytes=VMEM_BYTES),
    )(*results)
    return (results[0][None], results[1][None], results[2][None], results[3])


def body(gate_input, conv_input, grad_output, kernel):
    _, rows, channels = conv_input.shape
    groups, lag_count = kernel.shape
    peers = lax.axis_size("dp") * lax.axis_size("ctx")
    fits = (
        lax.axis_size("ctx") == 2
        and rows == TILE
        and lag_count == 2 * rows
        and channels % (2 * TILE) == 0
        and TILE % (channels // groups) == 0
        and lag_count % peers == 0
        and rows % (lag_count // peers) == 0
        and groups * (lag_count // peers) == 8 * TILE
    )
    if fits:
        return fused_body(gate_input, conv_input, grad_output, kernel)
    return general_body(gate_input, conv_input, grad_output, kernel)


def solution(mesh):
    return jax.shard_map(
        body,
        mesh=mesh,
        in_specs=(P("dp", "ctx", "ch"), P("dp", "ctx", "ch"), P("dp", "ctx", "ch"), P("ch", None)),
        out_specs=(
            P("dp", "ctx", "ch"),
            P("dp", "ctx", "ch"),
            P("dp", "ctx", "ch"),
            P("ch", ("dp", "ctx")),
        ),
        check_vma=False,
    )
```

```python
import functools
import math

import jax
import jax.numpy as jnp
from jax import lax
from jax.experimental import pallas as pl
from jax.experimental.pallas import tpu as pltpu
from jax.sharding import PartitionSpec as P


def toeplitz(padded_kernel, offset, tok_rows):
    groups = padded_kernel.shape[0]
    segment = lax.dynamic_slice_in_dim(padded_kernel, offset * tok_rows + 1, 2 * tok_rows, 1)
    reverse = segment[:, ::-1]
    rolled = jnp.concatenate([reverse[:, tok_rows:], reverse[:, :tok_rows]], axis=1)
    tiled = jnp.tile(rolled, (1, tok_rows))[:, : tok_rows * (2 * tok_rows - 1)]
    return tiled.reshape(groups, tok_rows, 2 * tok_rows - 1)[:, :, :tok_rows]


def diagonal_sums(matrix):
    groups = matrix.shape[0]
    extent = matrix.shape[1]
    flipped = matrix[:, :, ::-1]
    padded = jnp.pad(flipped, ((0, 0), (0, 0), (0, extent)))
    flattened = padded.reshape(groups, 2 * extent * extent)[:, : extent * (2 * extent - 1)]
    totals = jnp.sum(flattened.reshape(groups, extent, 2 * extent - 1), axis=1, dtype=jnp.float32)
    return jnp.pad(totals, ((0, 0), (0, 1)))


def general_body(gate_input, conv_input, grad_output, kernel):
    tok_rows = gate_input.shape[1]
    channels = gate_input.shape[2]
    groups = kernel.shape[0]
    group_size = channels // groups
    lag_count = kernel.shape[1]
    lag_blocks = lag_count // tok_rows
    padded_kernel = jnp.pad(kernel, ((0, 0), (tok_rows, 2 * tok_rows)))
    blocks = lax.axis_size("ctx")
    own_block = lax.axis_index("ctx")
    gate_rows = gate_input[0]
    grad_rows = grad_output[0]
    grad_mixed = (gate_rows.astype(jnp.float32) * grad_rows.astype(jnp.float32)).astype(
        jnp.bfloat16
    )

    def forward_add(running, matrix, block):
        shaped = block.reshape(tok_rows, groups, group_size)
        return running + jnp.einsum(
            "gab,bgc->agc", matrix, shaped, preferred_element_type=jnp.float32
        ).reshape(tok_rows, channels)

    def backward_add(running, matrix, block):
        shaped = block.reshape(tok_rows, groups, group_size)
        return running + jnp.einsum(
            "gab,agc->bgc", matrix, shaped, preferred_element_type=jnp.float32
        ).reshape(tok_rows, channels)

    def window_add(buffer, grad_block, value_block, offset):
        left_side = grad_block.reshape(tok_rows, groups, group_size)
        right_side = value_block.reshape(tok_rows, groups, group_size)
        paired = jnp.einsum(
            "agc,bgc->gab", left_side, right_side, preferred_element_type=jnp.float32
        ).astype(jnp.bfloat16)
        window = diagonal_sums(paired)
        first_col = offset * tok_rows
        current = lax.dynamic_slice_in_dim(buffer, first_col, 2 * tok_rows, 1)
        return lax.dynamic_update_slice_in_dim(buffer, current + window, first_col, 1)

    def visit_block(carried, value_block, grad_block, offset, has_value, has_grad):
        convolved, grad_vals, buffer = carried
        bounded = jnp.minimum(offset, lag_blocks)
        matrix = toeplitz(padded_kernel, bounded, tok_rows)
        convolved = lax.cond(
            has_value, lambda: forward_add(convolved, matrix, value_block), lambda: convolved
        )
        grad_vals = lax.cond(
            has_grad, lambda: backward_add(grad_vals, matrix, grad_block), lambda: grad_vals
        )
        buffer = lax.cond(
            has_value, lambda: window_add(buffer, grad_mixed, value_block, bounded), lambda: buffer
        )
        return (convolved, grad_vals, buffer)

    initial = (
        jnp.zeros((tok_rows, channels), jnp.float32),
        jnp.zeros((tok_rows, channels), jnp.float32),
        jnp.zeros((groups, lag_count + 2 * tok_rows), jnp.float32),
    )
    value_shard = lax.all_gather(conv_input, "ctx", axis=1, tiled=True)
    grad_shard = lax.all_gather(grad_mixed[None], "ctx", axis=1, tiled=True)
    pieces = value_shard.shape[1] // tok_rows

    def per_block(position, carried_now):
        value_block = lax.dynamic_slice_in_dim(value_shard[0], position * tok_rows, tok_rows, 0)
        grad_block = lax.dynamic_slice_in_dim(grad_shard[0], position * tok_rows, tok_rows, 0)
        distance = jnp.abs(own_block - position)
        near = distance <= lag_blocks
        return visit_block(
            carried_now,
            value_block,
            grad_block,
            distance,
            (position <= own_block) & near,
            (position >= own_block) & near,
        )

    carried = lax.fori_loop(0, pieces, per_block, initial)
    convolved, grad_vals, buffer = carried
    output = (gate_rows.astype(jnp.float32) * convolved).astype(jnp.bfloat16)[None]
    grad_gate = (grad_rows.astype(jnp.float32) * convolved).astype(jnp.bfloat16)[None]
    grad_conv = grad_vals.astype(jnp.bfloat16)[None]
    partial_value = buffer[:, tok_rows - 1 : tok_rows - 1 + lag_count]
    summed = lax.psum_scatter(partial_value, ("dp", "ctx"), scatter_dimension=1, tiled=True)
    grad_kernel = summed / math.sqrt(lax.axis_size("dp") * tok_rows * blocks)
    return (output, grad_gate, grad_conv, grad_kernel)


TILE = 128
VMEM_BYTES = 53 * 1024 * 1024
F32, BF16 = jnp.float32, jnp.bfloat16
MESH = pl.DeviceIdType.MESH


def dot(left, right):
    return jnp.dot(left, right, preferred_element_type=F32)


def dot_lanes(left, right):
    return lax.dot_general(left, right, (((1,), (1,)), ((), ())), preferred_element_type=F32)


def iota(shape, dim):
    return lax.broadcasted_iota(jnp.int32, shape, dim)


def fused_kernel(
    peers, scale,
    gate_hbm, conv_hbm, grad_hbm, taps_hbm,
    out_ref, ggate_ref, gconv_ref, gkern_ref,
    gate_ref, conv_ref, grad_ref, taps_ref, mixed, flipped, flipped_x, landed, other_x, other_g, zx, zg, turned_out, rev_taps, mats, part, packed, arrived,
    load_sem, save_sem, block_send, block_recv, sum_send, sum_recv,
):
    rows, channels = conv_ref.shape
    groups = taps_ref.shape[0]
    size = channels // groups
    per_tile = TILE // size
    tiles = channels // TILE
    half = tiles // 2
    dp, ctx = lax.axis_index("dp"), lax.axis_index("ctx")
    me = dp * 2 + ctx
    share = gkern_ref.shape[1]

    def place(index):
        return {"dp": index // 2, "ctx": lax.rem(index, 2)}

    loads = [
        pltpu.make_async_copy(source, target, load_sem.at[i])
        for i, (source, target) in enumerate(
            [(taps_hbm, taps_ref), (gate_hbm, gate_ref), (grad_hbm, grad_ref), (conv_hbm, conv_ref)]
        )
    ]
    for load in loads:
        load.start()

    barrier = pltpu.get_barrier_semaphore()
    for step in range(1, peers):
        pl.semaphore_signal(barrier, inc=1, device_id=place(lax.rem(me + step, peers)), device_id_type=MESH)

    row, col = iota((rows, rows), 0), iota((rows, rows), 1)
    lower = row >= col
    upper = row + col >= rows - 1
    backwards = jnp.where(row + col == rows - 1, 1.0, 0.0).astype(BF16)
    wrapped = jnp.where(lax.rem(row + col, rows) == 0, 1.0, 0.0).astype(BF16)
    loads[0].wait()
    rev_taps[0] = dot(taps_ref[:, :rows], wrapped)
    rev_taps[1] = dot(taps_ref[:, rows:], wrapped)

    lane = iota((1, TILE), 1)
    both = lax.rem(iota((1, 2 * TILE), 1), TILE)
    masks = [((lane // size) == q).astype(F32).astype(BF16) for q in range(per_tile)]

    def lanes(tile):
        start = tile * TILE
        return pl.ds(start if isinstance(tile, int) else pl.multiple_of(start, TILE), TILE)

    def build(tile):
        for q in range(per_tile):
            group = pl.ds(tile * per_tile + q, 1)
            near, far = [
                pltpu.roll(jnp.broadcast_to(rev_taps[h, group, :], (rows, rows)), 0, 1, stride=1, stride_axis=0)
                for h in range(2)
            ]
            mats[tile, q * rows : (q + 1) * rows, :rows] = jnp.where(lower, near, 0.0).astype(BF16)
            mats[tile, q * rows : (q + 1) * rows, rows:] = jnp.where(lower, far, near).astype(BF16)

    def diagonals(matrix):
        turned = pltpu.roll(matrix, 0, 1, stride=1, stride_axis=0)
        return jnp.sum(turned, axis=0, keepdims=True)

    def masked(block):
        return jnp.concatenate([block * m for m in masks], axis=0)

    def pairs(tile):
        return dot_lanes(masked(flipped_x[:, lanes(tile)]), mixed[:, lanes(tile)])

    def near_only(step):
        tile = (1 - ctx) * half + step
        found = pairs(tile)
        for q in range(per_tile):
            group = pl.ds(tile * per_tile + q, 1)
            part[0, group, :] = diagonals(jnp.where(upper, found[q * rows : (q + 1) * rows], 0.0))
            part[1, group, :] = jnp.zeros((1, rows), F32)

    def near_and_far(step):
        tile = ctx * half + step
        found = pairs(tile)
        across = dot_lanes(masked(other_x[:, lanes(tile)]), other_g[:, lanes(tile)])
        for q in range(per_tile):
            group = pl.ds(tile * per_tile + q, 1)
            inner, outer = found[q * rows : (q + 1) * rows], across[q * rows : (q + 1) * rows]
            part[0, group, :] = diagonals(jnp.where(upper, inner, outer))
            part[1, group, :] = diagonals(jnp.where(upper, outer, 0.0))

    for tile in range(half):
        build(tile)
    for load in loads[1:]:
        load.wait()
    mixed[...] = (gate_ref[...].astype(F32) * grad_ref[...].astype(F32)).astype(BF16)

    pl.semaphore_wait(barrier, peers - 1)
    partner = {"ctx": 1 - ctx}

    def exchange(source):
        return pltpu.make_async_remote_copy(
            src_ref=source, dst_ref=landed, send_sem=block_send, recv_sem=block_recv,
            device_id=partner, device_id_type=MESH,
        )

    @pl.when(ctx == 0)
    def _():
        exchange(conv_ref).start()

    @pl.when(ctx == 1)
    def _():
        exchange(mixed).start()

    flipped_x[...] = dot(backwards, conv_ref[...]).astype(BF16)
    flipped[...] = dot(backwards, mixed[...]).astype(BF16)
    for step in range(half):
        near_only(step)

    exchange(conv_ref).wait_recv()
    block = landed[...]
    turned_block = dot(backwards, block).astype(BF16)
    first = ctx == 0
    other_x[...] = jnp.where(first, flipped_x[...], turned_block)
    other_g[...] = jnp.where(first, block, mixed[...])
    for step in range(half):
        near_and_far(step)

    for peer in range(peers):
        h, e = peer // (rows // share), peer % (rows // share)
        tile8 = jnp.zeros((8, TILE), F32)
        for j in range(groups // 8):
            value = part[h, 8 * j : 8 * j + 8, :]
            shift = (share * (j - e) + 1) % TILE
            if shift:
                value = pltpu.roll(value, shift, 1)
            tile8 = jnp.where(lane // share == j, value, tile8)
        packed[peer] = tile8

    def send_sum(step):
        peer = lax.rem(me + step, peers)
        return pltpu.make_async_remote_copy(
            src_ref=packed.at[peer], dst_ref=arrived.at[step],
            send_sem=sum_send.at[step], recv_sem=sum_recv.at[step],
            device_id=place(peer), device_id_type=MESH,
        )

    copies = [send_sum(step) for step in range(1, peers)]
    for copy in copies:
        copy.start()

    zx[...] = jnp.where(first, jnp.zeros_like(block), block)
    zg[...] = jnp.where(first, turned_block, jnp.zeros_like(block))

    def convolve(tile):
        at = lanes(tile)
        stacked = jnp.concatenate(
            [
                jnp.concatenate([conv_ref[:, at], flipped[:, at]], axis=1),
                jnp.concatenate([zx[:, at], zg[:, at]], axis=1),
            ],
            axis=0,
        )
        every = dot(mats[tile], stacked)
        total = every[:rows]
        for q in range(1, per_tile):
            total = jnp.where(both // size == q, every[q * rows : (q + 1) * rows], total)
        convolved = total[:, :TILE]
        out_ref[:, at] = (gate_ref[:, at].astype(F32) * convolved).astype(BF16)
        ggate_ref[:, at] = (grad_ref[:, at].astype(F32) * convolved).astype(BF16)
        turned_out[:, at] = total[:, TILE:].astype(BF16)

    saves = []
    for part_index in range(2):
        for tile in range(part_index * half, (part_index + 1) * half):
            if part_index == 0:
                build(tile + half)
            convolve(tile)
        at = slice(part_index * half * TILE, (part_index + 1) * half * TILE)
        gconv_ref[:, at] = dot(backwards, turned_out[:, at]).astype(BF16)

    exchange(conv_ref).wait_send()
    summed = packed[me]
    for step, copy in zip(range(1, peers), copies):
        copy.wait()
        summed = summed + arrived[step]
    summed = summed * scale
    for j in range(groups // 8):
        value = summed if j == 0 else pltpu.roll(summed, TILE - share * j, 1)
        gkern_ref[8 * j : 8 * j + 8, :] = value[:, :share]
    for save in saves:
        save.wait()


def store_kernel(*refs):
    sems = refs[-1]
    copies = [pltpu.make_async_copy(refs[i], refs[4 + i], sems.at[i]) for i in range(4)]
    for copy in copies:
        copy.start()
    for copy in copies:
        copy.wait()


def fused_body(gate_input, conv_input, grad_output, kernel):
    _, rows, channels = conv_input.shape
    groups, lag_count = kernel.shape
    tiles = channels // TILE
    peers = lax.axis_size("dp") * lax.axis_size("ctx")
    scale = 1.0 / math.sqrt(lax.axis_size("dp") * rows * lax.axis_size("ctx"))
    block = jax.ShapeDtypeStruct((rows, channels), BF16)
    vmem = pl.BlockSpec(memory_space=pltpu.VMEM)
    hbm = pl.BlockSpec(memory_space=pltpu.HBM)
    results = pl.pallas_call(
        functools.partial(fused_kernel, peers, scale),
        out_shape=[block, block, block, jax.ShapeDtypeStruct((groups, lag_count // peers), F32)],
        in_specs=[hbm] * 4,
        out_specs=[vmem] * 4,
        scratch_shapes=[pltpu.VMEM((rows, channels), BF16)] * 3
        + [pltpu.VMEM((groups, lag_count), BF16)]
        + [pltpu.VMEM((rows, channels), BF16)] * 9
        + [
            pltpu.VMEM((2, groups, rows), F32),
            pltpu.VMEM((tiles, (groups // tiles) * rows, 2 * rows), BF16),
            pltpu.VMEM((2, groups, rows), F32),
            pltpu.VMEM((peers, 8, TILE), F32),
            pltpu.VMEM((peers, 8, TILE), F32),
            pltpu.SemaphoreType.DMA((4,)),
            pltpu.SemaphoreType.DMA((2, 3)),
            pltpu.SemaphoreType.DMA,
            pltpu.SemaphoreType.DMA,
            pltpu.SemaphoreType.DMA((peers,)),
            pltpu.SemaphoreType.DMA((peers,)),
        ],
        compiler_params=pltpu.CompilerParams(
            collective_id=0, has_side_effects=True, vmem_limit_bytes=VMEM_BYTES
        ),
        cost_estimate=pl.CostEstimate(
            flops=20 * rows * rows * channels, bytes_accessed=12 * rows * channels, transcendentals=0
        ),
    )(gate_input[0], conv_input[0], grad_output[0], kernel)
    results = pl.pallas_call(
        store_kernel,
        out_shape=[block, block, block, jax.ShapeDtypeStruct((groups, lag_count // peers), F32)],
        in_specs=[vmem] * 4,
        out_specs=[hbm] * 4,
        scratch_shapes=[pltpu.SemaphoreType.DMA((4,))],
        compiler_params=pltpu.CompilerParams(vmem_limit_bytes=VMEM_BYTES),
    )(*results)
    return (results[0][None], results[1][None], results[2][None], results[3])


def body(gate_input, conv_input, grad_output, kernel):
    _, rows, channels = conv_input.shape
    groups, lag_count = kernel.shape
    peers = lax.axis_size("dp") * lax.axis_size("ctx")
    fits = (
        lax.axis_size("ctx") == 2
        and rows == TILE
        and lag_count == 2 * rows
        and channels % (2 * TILE) == 0
        and TILE % (channels // groups) == 0
        and lag_count % peers == 0
        and rows % (lag_count // peers) == 0
        and groups * (lag_count // peers) == 8 * TILE
    )
    if fits:
        return fused_body(gate_input, conv_input, grad_output, kernel)
    return general_body(gate_input, conv_input, grad_output, kernel)


def solution(mesh):
    return jax.shard_map(
        body,
        mesh=mesh,
        in_specs=(P("dp", "ctx", "ch"), P("dp", "ctx", "ch"), P("dp", "ctx", "ch"), P("ch", None)),
        out_specs=(
            P("dp", "ctx", "ch"),
            P("dp", "ctx", "ch"),
            P("dp", "ctx", "ch"),
            P("ch", ("dp", "ctx")),
        ),
        check_vma=False,
    )
```

```python
import functools
import math

import jax
import jax.numpy as jnp
from jax import lax
from jax.experimental import pallas as pl
from jax.experimental.pallas import tpu as pltpu
from jax.sharding import PartitionSpec as P


def toeplitz(padded_kernel, offset, tok_rows):
    groups = padded_kernel.shape[0]
    segment = lax.dynamic_slice_in_dim(padded_kernel, offset * tok_rows + 1, 2 * tok_rows, 1)
    reverse = segment[:, ::-1]
    rolled = jnp.concatenate([reverse[:, tok_rows:], reverse[:, :tok_rows]], axis=1)
    tiled = jnp.tile(rolled, (1, tok_rows))[:, : tok_rows * (2 * tok_rows - 1)]
    return tiled.reshape(groups, tok_rows, 2 * tok_rows - 1)[:, :, :tok_rows]


def diagonal_sums(matrix):
    groups = matrix.shape[0]
    extent = matrix.shape[1]
    flipped = matrix[:, :, ::-1]
    padded = jnp.pad(flipped, ((0, 0), (0, 0), (0, extent)))
    flattened = padded.reshape(groups, 2 * extent * extent)[:, : extent * (2 * extent - 1)]
    totals = jnp.sum(flattened.reshape(groups, extent, 2 * extent - 1), axis=1, dtype=jnp.float32)
    return jnp.pad(totals, ((0, 0), (0, 1)))


def general_body(gate_input, conv_input, grad_output, kernel):
    tok_rows = gate_input.shape[1]
    channels = gate_input.shape[2]
    groups = kernel.shape[0]
    group_size = channels // groups
    lag_count = kernel.shape[1]
    lag_blocks = lag_count // tok_rows
    padded_kernel = jnp.pad(kernel, ((0, 0), (tok_rows, 2 * tok_rows)))
    blocks = lax.axis_size("ctx")
    own_block = lax.axis_index("ctx")
    gate_rows = gate_input[0]
    grad_rows = grad_output[0]
    grad_mixed = (gate_rows.astype(jnp.float32) * grad_rows.astype(jnp.float32)).astype(
        jnp.bfloat16
    )

    def forward_add(running, matrix, block):
        shaped = block.reshape(tok_rows, groups, group_size)
        return running + jnp.einsum(
            "gab,bgc->agc", matrix, shaped, preferred_element_type=jnp.float32
        ).reshape(tok_rows, channels)

    def backward_add(running, matrix, block):
        shaped = block.reshape(tok_rows, groups, group_size)
        return running + jnp.einsum(
            "gab,agc->bgc", matrix, shaped, preferred_element_type=jnp.float32
        ).reshape(tok_rows, channels)

    def window_add(buffer, grad_block, value_block, offset):
        left_side = grad_block.reshape(tok_rows, groups, group_size)
        right_side = value_block.reshape(tok_rows, groups, group_size)
        paired = jnp.einsum(
            "agc,bgc->gab", left_side, right_side, preferred_element_type=jnp.float32
        ).astype(jnp.bfloat16)
        window = diagonal_sums(paired)
        first_col = offset * tok_rows
        current = lax.dynamic_slice_in_dim(buffer, first_col, 2 * tok_rows, 1)
        return lax.dynamic_update_slice_in_dim(buffer, current + window, first_col, 1)

    def visit_block(carried, value_block, grad_block, offset, has_value, has_grad):
        convolved, grad_vals, buffer = carried
        bounded = jnp.minimum(offset, lag_blocks)
        matrix = toeplitz(padded_kernel, bounded, tok_rows)
        convolved = lax.cond(
            has_value, lambda: forward_add(convolved, matrix, value_block), lambda: convolved
        )
        grad_vals = lax.cond(
            has_grad, lambda: backward_add(grad_vals, matrix, grad_block), lambda: grad_vals
        )
        buffer = lax.cond(
            has_value, lambda: window_add(buffer, grad_mixed, value_block, bounded), lambda: buffer
        )
        return (convolved, grad_vals, buffer)

    initial = (
        jnp.zeros((tok_rows, channels), jnp.float32),
        jnp.zeros((tok_rows, channels), jnp.float32),
        jnp.zeros((groups, lag_count + 2 * tok_rows), jnp.float32),
    )
    value_shard = lax.all_gather(conv_input, "ctx", axis=1, tiled=True)
    grad_shard = lax.all_gather(grad_mixed[None], "ctx", axis=1, tiled=True)
    pieces = value_shard.shape[1] // tok_rows

    def per_block(position, carried_now):
        value_block = lax.dynamic_slice_in_dim(value_shard[0], position * tok_rows, tok_rows, 0)
        grad_block = lax.dynamic_slice_in_dim(grad_shard[0], position * tok_rows, tok_rows, 0)
        distance = jnp.abs(own_block - position)
        near = distance <= lag_blocks
        return visit_block(
            carried_now,
            value_block,
            grad_block,
            distance,
            (position <= own_block) & near,
            (position >= own_block) & near,
        )

    carried = lax.fori_loop(0, pieces, per_block, initial)
    convolved, grad_vals, buffer = carried
    output = (gate_rows.astype(jnp.float32) * convolved).astype(jnp.bfloat16)[None]
    grad_gate = (grad_rows.astype(jnp.float32) * convolved).astype(jnp.bfloat16)[None]
    grad_conv = grad_vals.astype(jnp.bfloat16)[None]
    partial_value = buffer[:, tok_rows - 1 : tok_rows - 1 + lag_count]
    summed = lax.psum_scatter(partial_value, ("dp", "ctx"), scatter_dimension=1, tiled=True)
    grad_kernel = summed / math.sqrt(lax.axis_size("dp") * tok_rows * blocks)
    return (output, grad_gate, grad_conv, grad_kernel)


TILE = 128
VMEM_BYTES = 53 * 1024 * 1024
F32, BF16 = jnp.float32, jnp.bfloat16
MESH = pl.DeviceIdType.MESH


def dot(left, right):
    return jnp.dot(left, right, preferred_element_type=F32)


def dot_lanes(left, right):
    return lax.dot_general(left, right, (((1,), (1,)), ((), ())), preferred_element_type=F32)


def iota(shape, dim):
    return lax.broadcasted_iota(jnp.int32, shape, dim)


def fused_kernel(
    peers, scale,
    gate_hbm, conv_hbm, grad_hbm, taps_hbm,
    out_ref, ggate_ref, gconv_ref, gkern_ref,
    gate_ref, conv_ref, grad_ref, taps_ref, mixed, flipped, flipped_x, landed, zx, zg, turned_out, rev_taps, mats, part, packed, arrived,
    load_sem, save_sem, block_send, block_recv, sum_send, sum_recv,
):
    rows, channels = conv_ref.shape
    groups = taps_ref.shape[0]
    size = channels // groups
    per_tile = TILE // size
    tiles = channels // TILE
    half = tiles // 2
    dp, ctx = lax.axis_index("dp"), lax.axis_index("ctx")
    me = dp * 2 + ctx
    share = gkern_ref.shape[1]

    def place(index):
        return {"dp": index // 2, "ctx": lax.rem(index, 2)}

    loads = [
        pltpu.make_async_copy(source, target, load_sem.at[i])
        for i, (source, target) in enumerate(
            [(taps_hbm, taps_ref), (gate_hbm, gate_ref), (grad_hbm, grad_ref), (conv_hbm, conv_ref)]
        )
    ]
    for load in loads:
        load.start()

    barrier = pltpu.get_barrier_semaphore()
    for step in range(1, peers):
        pl.semaphore_signal(barrier, inc=1, device_id=place(lax.rem(me + step, peers)), device_id_type=MESH)

    row, col = iota((rows, rows), 0), iota((rows, rows), 1)
    lower = row >= col
    upper = row + col >= rows - 1
    backwards = jnp.where(row + col == rows - 1, 1.0, 0.0).astype(BF16)
    wrapped = jnp.where(lax.rem(row + col, rows) == 0, 1.0, 0.0).astype(BF16)
    loads[0].wait()
    rev_taps[0] = dot(taps_ref[:, :rows], wrapped)
    rev_taps[1] = dot(taps_ref[:, rows:], wrapped)

    lane = iota((1, TILE), 1)
    both = lax.rem(iota((1, 2 * TILE), 1), TILE)
    masks = [((lane // size) == q).astype(F32).astype(BF16) for q in range(per_tile)]

    def lanes(tile):
        start = tile * TILE
        return pl.ds(start if isinstance(tile, int) else pl.multiple_of(start, TILE), TILE)

    def build(tile):
        for q in range(per_tile):
            group = pl.ds(tile * per_tile + q, 1)
            near, far = [
                pltpu.roll(jnp.broadcast_to(rev_taps[h, group, :], (rows, rows)), 0, 1, stride=1, stride_axis=0)
                for h in range(2)
            ]
            mats[tile, q * rows : (q + 1) * rows, :rows] = jnp.where(lower, near, 0.0).astype(BF16)
            mats[tile, q * rows : (q + 1) * rows, rows:] = jnp.where(lower, far, near).astype(BF16)

    def diagonals(matrix):
        turned = pltpu.roll(matrix, 0, 1, stride=1, stride_axis=0)
        return jnp.sum(turned, axis=0, keepdims=True)

    def masked(block):
        return jnp.concatenate([block * m for m in masks], axis=0)

    def pairs(tile):
        return dot_lanes(masked(flipped_x[:, lanes(tile)]), mixed[:, lanes(tile)])

    def near_only(step):
        tile = (1 - ctx) * half + step
        found = pairs(tile)
        for q in range(per_tile):
            group = pl.ds(tile * per_tile + q, 1)
            part[0, group, :] = diagonals(jnp.where(upper, found[q * rows : (q + 1) * rows], 0.0))
            part[1, group, :] = jnp.zeros((1, rows), F32)

    def near_and_far(step):
        tile = ctx * half + step
        found = pairs(tile)
        own_x, own_g, block = flipped_x[:, lanes(tile)], mixed[:, lanes(tile)], landed[:, lanes(tile)]
        across = dot_lanes(masked(jnp.where(first, own_x, block)), jnp.where(first, block, own_g))
        for q in range(per_tile):
            group = pl.ds(tile * per_tile + q, 1)
            inner, outer = found[q * rows : (q + 1) * rows], across[q * rows : (q + 1) * rows]
            part[0, group, :] = diagonals(jnp.where(upper, inner, outer))
            part[1, group, :] = diagonals(jnp.where(upper, outer, 0.0))

    for tile in range(half):
        build(tile)
    for load in loads[1:]:
        load.wait()
    def prepare(at):
        flipped_x[:, at] = dot(backwards, conv_ref[:, at]).astype(BF16)
        mixed[:, at] = (gate_ref[:, at].astype(F32) * grad_ref[:, at].astype(F32)).astype(BF16)

    def columns(first_tile, count):
        return pl.ds(pl.multiple_of(first_tile * TILE, TILE), count * TILE)

    quarter = half // 2
    pieces = [
        columns((1 - ctx) * half, quarter),
        columns((1 - ctx) * half + quarter, quarter),
        columns(ctx * half, half),
    ]
    partner = {"ctx": 1 - ctx}

    def exchange(source, piece):
        return pltpu.make_async_remote_copy(
            src_ref=source.at[:, pieces[piece]], dst_ref=landed.at[:, pieces[piece]],
            send_sem=block_send.at[piece], recv_sem=block_recv.at[piece],
            device_id=partner, device_id_type=MESH,
        )

    def send(piece):
        @pl.when(ctx == 0)
        def _():
            exchange(flipped_x, piece).start()

        @pl.when(ctx == 1)
        def _():
            exchange(mixed, piece).start()

    prepare(columns((1 - ctx) * half, half))
    pl.semaphore_wait(barrier, peers - 1)
    send(0)
    send(1)
    prepare(columns(ctx * half, half))
    send(2)

    flipped[...] = dot(backwards, mixed[...]).astype(BF16)
    for step in range(half):
        near_only(step)

    first = ctx == 0
    for step in range(half):
        if step % quarter == 0:
            exchange(mixed, step // quarter).wait_recv()
        near_and_far(step)

    for peer in range(peers):
        h, e = peer // (rows // share), peer % (rows // share)
        tile8 = jnp.zeros((8, TILE), F32)
        for j in range(groups // 8):
            value = part[h, 8 * j : 8 * j + 8, :]
            shift = (share * (j - e) + 1) % TILE
            if shift:
                value = pltpu.roll(value, shift, 1)
            tile8 = jnp.where(lane // share == j, value, tile8)
        packed[peer] = tile8

    def send_sum(step):
        peer = lax.rem(me + step, peers)
        return pltpu.make_async_remote_copy(
            src_ref=packed.at[peer], dst_ref=arrived.at[step],
            send_sem=sum_send.at[step], recv_sem=sum_recv.at[step],
            device_id=place(peer), device_id_type=MESH,
        )

    copies = [send_sum(step) for step in range(1, peers)]
    for copy in copies:
        copy.start()

    exchange(mixed, 2).wait_recv()
    turned_block = dot(backwards, landed[...]).astype(BF16)
    zx[...] = jnp.where(first, jnp.zeros_like(turned_block), turned_block)
    zg[...] = jnp.where(first, turned_block, jnp.zeros_like(turned_block))

    def convolve(tile):
        at = lanes(tile)
        stacked = jnp.concatenate(
            [
                jnp.concatenate([conv_ref[:, at], flipped[:, at]], axis=1),
                jnp.concatenate([zx[:, at], zg[:, at]], axis=1),
            ],
            axis=0,
        )
        every = dot(mats[tile], stacked)
        total = every[:rows]
        for q in range(1, per_tile):
            total = jnp.where(both // size == q, every[q * rows : (q + 1) * rows], total)
        convolved = total[:, :TILE]
        out_ref[:, at] = (gate_ref[:, at].astype(F32) * convolved).astype(BF16)
        ggate_ref[:, at] = (grad_ref[:, at].astype(F32) * convolved).astype(BF16)
        turned_out[:, at] = total[:, TILE:].astype(BF16)

    saves = []
    for part_index in range(2):
        for tile in range(part_index * half, (part_index + 1) * half):
            if part_index == 0:
                build(tile + half)
            convolve(tile)
        at = slice(part_index * half * TILE, (part_index + 1) * half * TILE)
        gconv_ref[:, at] = dot(backwards, turned_out[:, at]).astype(BF16)

    for piece in range(3):
        exchange(mixed, piece).wait_send()
    summed = packed[me]
    for step, copy in zip(range(1, peers), copies):
        copy.wait()
        summed = summed + arrived[step]
    summed = summed * scale
    for j in range(groups // 8):
        value = summed if j == 0 else pltpu.roll(summed, TILE - share * j, 1)
        gkern_ref[8 * j : 8 * j + 8, :] = value[:, :share]
    for save in saves:
        save.wait()


def store_kernel(*refs):
    sems = refs[-1]
    copies = [pltpu.make_async_copy(refs[i], refs[4 + i], sems.at[i]) for i in range(4)]
    for copy in copies:
        copy.start()
    for copy in copies:
        copy.wait()


def fused_body(gate_input, conv_input, grad_output, kernel):
    _, rows, channels = conv_input.shape
    groups, lag_count = kernel.shape
    tiles = channels // TILE
    peers = lax.axis_size("dp") * lax.axis_size("ctx")
    scale = 1.0 / math.sqrt(lax.axis_size("dp") * rows * lax.axis_size("ctx"))
    block = jax.ShapeDtypeStruct((rows, channels), BF16)
    vmem = pl.BlockSpec(memory_space=pltpu.VMEM)
    hbm = pl.BlockSpec(memory_space=pltpu.HBM)
    results = pl.pallas_call(
        functools.partial(fused_kernel, peers, scale),
        out_shape=[block, block, block, jax.ShapeDtypeStruct((groups, lag_count // peers), F32)],
        in_specs=[hbm] * 4,
        out_specs=[vmem] * 4,
        scratch_shapes=[pltpu.VMEM((rows, channels), BF16)] * 3
        + [pltpu.VMEM((groups, lag_count), BF16)]
        + [pltpu.VMEM((rows, channels), BF16)] * 7
        + [
            pltpu.VMEM((2, groups, rows), F32),
            pltpu.VMEM((tiles, (groups // tiles) * rows, 2 * rows), BF16),
            pltpu.VMEM((2, groups, rows), F32),
            pltpu.VMEM((peers, 8, TILE), F32),
            pltpu.VMEM((peers, 8, TILE), F32),
            pltpu.SemaphoreType.DMA((4,)),
            pltpu.SemaphoreType.DMA((2, 3)),
            pltpu.SemaphoreType.DMA((3,)),
            pltpu.SemaphoreType.DMA((3,)),
            pltpu.SemaphoreType.DMA((peers,)),
            pltpu.SemaphoreType.DMA((peers,)),
        ],
        compiler_params=pltpu.CompilerParams(
            collective_id=0, has_side_effects=True, vmem_limit_bytes=VMEM_BYTES
        ),
        cost_estimate=pl.CostEstimate(
            flops=20 * rows * rows * channels, bytes_accessed=12 * rows * channels, transcendentals=0
        ),
    )(gate_input[0], conv_input[0], grad_output[0], kernel)
    results = pl.pallas_call(
        store_kernel,
        out_shape=[block, block, block, jax.ShapeDtypeStruct((groups, lag_count // peers), F32)],
        in_specs=[vmem] * 4,
        out_specs=[hbm] * 4,
        scratch_shapes=[pltpu.SemaphoreType.DMA((4,))],
        compiler_params=pltpu.CompilerParams(vmem_limit_bytes=VMEM_BYTES),
    )(*results)
    return (results[0][None], results[1][None], results[2][None], results[3])


def body(gate_input, conv_input, grad_output, kernel):
    _, rows, channels = conv_input.shape
    groups, lag_count = kernel.shape
    peers = lax.axis_size("dp") * lax.axis_size("ctx")
    fits = (
        lax.axis_size("ctx") == 2
        and rows == TILE
        and lag_count == 2 * rows
        and channels % (2 * TILE) == 0
        and TILE % (channels // groups) == 0
        and lag_count % peers == 0
        and rows % (lag_count // peers) == 0
        and groups * (lag_count // peers) == 8 * TILE
    )
    if fits:
        return fused_body(gate_input, conv_input, grad_output, kernel)
    return general_body(gate_input, conv_input, grad_output, kernel)


def solution(mesh):
    return jax.shard_map(
        body,
        mesh=mesh,
        in_specs=(P("dp", "ctx", "ch"), P("dp", "ctx", "ch"), P("dp", "ctx", "ch"), P("ch", None)),
        out_specs=(
            P("dp", "ctx", "ch"),
            P("dp", "ctx", "ch"),
            P("dp", "ctx", "ch"),
            P("ch", ("dp", "ctx")),
        ),
        check_vma=False,
    )
```

```python
import functools
import math

import jax
import jax.numpy as jnp
from jax import lax
from jax.experimental import pallas as pl
from jax.experimental.pallas import tpu as pltpu
from jax.sharding import PartitionSpec as P


def toeplitz(padded_kernel, offset, tok_rows):
    groups = padded_kernel.shape[0]
    segment = lax.dynamic_slice_in_dim(padded_kernel, offset * tok_rows + 1, 2 * tok_rows, 1)
    reverse = segment[:, ::-1]
    rolled = jnp.concatenate([reverse[:, tok_rows:], reverse[:, :tok_rows]], axis=1)
    tiled = jnp.tile(rolled, (1, tok_rows))[:, : tok_rows * (2 * tok_rows - 1)]
    return tiled.reshape(groups, tok_rows, 2 * tok_rows - 1)[:, :, :tok_rows]


def diagonal_sums(matrix):
    groups = matrix.shape[0]
    extent = matrix.shape[1]
    flipped = matrix[:, :, ::-1]
    padded = jnp.pad(flipped, ((0, 0), (0, 0), (0, extent)))
    flattened = padded.reshape(groups, 2 * extent * extent)[:, : extent * (2 * extent - 1)]
    totals = jnp.sum(flattened.reshape(groups, extent, 2 * extent - 1), axis=1, dtype=jnp.float32)
    return jnp.pad(totals, ((0, 0), (0, 1)))


def general_body(gate_input, conv_input, grad_output, kernel):
    tok_rows = gate_input.shape[1]
    channels = gate_input.shape[2]
    groups = kernel.shape[0]
    group_size = channels // groups
    lag_count = kernel.shape[1]
    lag_blocks = lag_count // tok_rows
    padded_kernel = jnp.pad(kernel, ((0, 0), (tok_rows, 2 * tok_rows)))
    blocks = lax.axis_size("ctx")
    own_block = lax.axis_index("ctx")
    gate_rows = gate_input[0]
    grad_rows = grad_output[0]
    grad_mixed = (gate_rows.astype(jnp.float32) * grad_rows.astype(jnp.float32)).astype(
        jnp.bfloat16
    )

    def forward_add(running, matrix, block):
        shaped = block.reshape(tok_rows, groups, group_size)
        return running + jnp.einsum(
            "gab,bgc->agc", matrix, shaped, preferred_element_type=jnp.float32
        ).reshape(tok_rows, channels)

    def backward_add(running, matrix, block):
        shaped = block.reshape(tok_rows, groups, group_size)
        return running + jnp.einsum(
            "gab,agc->bgc", matrix, shaped, preferred_element_type=jnp.float32
        ).reshape(tok_rows, channels)

    def window_add(buffer, grad_block, value_block, offset):
        left_side = grad_block.reshape(tok_rows, groups, group_size)
        right_side = value_block.reshape(tok_rows, groups, group_size)
        paired = jnp.einsum(
            "agc,bgc->gab", left_side, right_side, preferred_element_type=jnp.float32
        ).astype(jnp.bfloat16)
        window = diagonal_sums(paired)
        first_col = offset * tok_rows
        current = lax.dynamic_slice_in_dim(buffer, first_col, 2 * tok_rows, 1)
        return lax.dynamic_update_slice_in_dim(buffer, current + window, first_col, 1)

    def visit_block(carried, value_block, grad_block, offset, has_value, has_grad):
        convolved, grad_vals, buffer = carried
        bounded = jnp.minimum(offset, lag_blocks)
        matrix = toeplitz(padded_kernel, bounded, tok_rows)
        convolved = lax.cond(
            has_value, lambda: forward_add(convolved, matrix, value_block), lambda: convolved
        )
        grad_vals = lax.cond(
            has_grad, lambda: backward_add(grad_vals, matrix, grad_block), lambda: grad_vals
        )
        buffer = lax.cond(
            has_value, lambda: window_add(buffer, grad_mixed, value_block, bounded), lambda: buffer
        )
        return (convolved, grad_vals, buffer)

    initial = (
        jnp.zeros((tok_rows, channels), jnp.float32),
        jnp.zeros((tok_rows, channels), jnp.float32),
        jnp.zeros((groups, lag_count + 2 * tok_rows), jnp.float32),
    )
    value_shard = lax.all_gather(conv_input, "ctx", axis=1, tiled=True)
    grad_shard = lax.all_gather(grad_mixed[None], "ctx", axis=1, tiled=True)
    pieces = value_shard.shape[1] // tok_rows

    def per_block(position, carried_now):
        value_block = lax.dynamic_slice_in_dim(value_shard[0], position * tok_rows, tok_rows, 0)
        grad_block = lax.dynamic_slice_in_dim(grad_shard[0], position * tok_rows, tok_rows, 0)
        distance = jnp.abs(own_block - position)
        near = distance <= lag_blocks
        return visit_block(
            carried_now,
            value_block,
            grad_block,
            distance,
            (position <= own_block) & near,
            (position >= own_block) & near,
        )

    carried = lax.fori_loop(0, pieces, per_block, initial)
    convolved, grad_vals, buffer = carried
    output = (gate_rows.astype(jnp.float32) * convolved).astype(jnp.bfloat16)[None]
    grad_gate = (grad_rows.astype(jnp.float32) * convolved).astype(jnp.bfloat16)[None]
    grad_conv = grad_vals.astype(jnp.bfloat16)[None]
    partial_value = buffer[:, tok_rows - 1 : tok_rows - 1 + lag_count]
    summed = lax.psum_scatter(partial_value, ("dp", "ctx"), scatter_dimension=1, tiled=True)
    grad_kernel = summed / math.sqrt(lax.axis_size("dp") * tok_rows * blocks)
    return (output, grad_gate, grad_conv, grad_kernel)


TILE = 128
STRIP = 16
VMEM_BYTES = 53 * 1024 * 1024
F32, BF16 = jnp.float32, jnp.bfloat16
MESH = pl.DeviceIdType.MESH


def dot(left, right):
    return jnp.dot(left, right, preferred_element_type=F32)


def dot_lanes(left, right):
    return lax.dot_general(left, right, (((1,), (1,)), ((), ())), preferred_element_type=F32)


def iota(shape, dim):
    return lax.broadcasted_iota(jnp.int32, shape, dim)


def fused_kernel(
    peers, scale,
    gate_hbm, conv_hbm, grad_hbm, taps_hbm,
    out_ref, ggate_ref, gconv_ref, gkern_ref,
    gate_ref, conv_ref, grad_ref, taps_ref, mixed, flipped, flipped_x, landed, zx, zg, turned_out, rev_taps, mats, part, packed, arrived,
    load_sem, save_sem, block_send, block_recv, sum_send, sum_recv,
):
    rows, channels = conv_ref.shape
    groups = taps_ref.shape[0]
    size = channels // groups
    per_tile = TILE // size
    tiles = channels // TILE
    half = tiles // 2
    dp, ctx = lax.axis_index("dp"), lax.axis_index("ctx")
    me = dp * 2 + ctx
    share = gkern_ref.shape[1]

    def place(index):
        return {"dp": index // 2, "ctx": lax.rem(index, 2)}

    loads = [
        pltpu.make_async_copy(source, target, load_sem.at[i])
        for i, (source, target) in enumerate(
            [(taps_hbm, taps_ref), (gate_hbm, gate_ref), (grad_hbm, grad_ref), (conv_hbm, conv_ref)]
        )
    ]
    for load in loads:
        load.start()

    barrier = pltpu.get_barrier_semaphore()
    for step in range(1, peers):
        pl.semaphore_signal(barrier, inc=1, device_id=place(lax.rem(me + step, peers)), device_id_type=MESH)

    row, col = iota((rows, rows), 0), iota((rows, rows), 1)
    upper = (row + col >= rows - 1).astype(F32).astype(BF16)
    beyond = (row + col < rows - 1).astype(F32).astype(BF16)
    backwards = jnp.where(row + col == rows - 1, 1.0, 0.0).astype(BF16)
    wrapped = jnp.where(lax.rem(row + col, rows) == 0, 1.0, 0.0).astype(BF16)
    loads[0].wait()
    rev_taps[0] = dot(taps_ref[:, :rows], wrapped)
    rev_taps[1] = dot(taps_ref[:, rows:], wrapped)

    lane = iota((1, TILE), 1)
    both = lax.rem(iota((1, 2 * TILE), 1), TILE)
    masks = [((lane // size) == q).astype(F32).astype(BF16) for q in range(per_tile)]

    def lanes(tile):
        start = tile * TILE
        return pl.ds(start if isinstance(tile, int) else pl.multiple_of(start, TILE), TILE)

    def bits(mask):
        return mask.astype(F32).astype(BF16)

    strips = rows // STRIP
    strip_row, strip_col = iota((STRIP, rows), 0), iota((STRIP, rows), 1)
    below = [bits(strip_row + n * STRIP >= strip_col) for n in range(strips)]
    above = [bits(strip_row + n * STRIP < strip_col) for n in range(strips)]

    def turn(strip, n):
        return pltpu.roll(strip, n * STRIP, 1) if n else strip

    def build(tile):
        for q in range(per_tile):
            group = pl.ds(tile * per_tile + q, 1)
            near, far = [
                pltpu.roll(
                    jnp.broadcast_to(rev_taps[h, group, :], (STRIP, rows)), 0, 1, stride=1, stride_axis=0
                ).astype(BF16)
                for h in range(2)
            ]
            for n in range(strips):
                at = slice(q * rows + n * STRIP, q * rows + (n + 1) * STRIP)
                near_n, far_n = turn(near, n), turn(far, n)
                mats[tile, at, :rows] = near_n * below[n]
                mats[tile, at, rows:] = far_n * below[n] + near_n * above[n]

    def diagonals(matrix):
        total = jnp.zeros((STRIP, rows), F32)
        for n in range(strips):
            total = total + turn(matrix[n * STRIP : (n + 1) * STRIP], n).astype(F32)
        turned = pltpu.roll(total, 0, 1, stride=1, stride_axis=0)
        return jnp.sum(turned, axis=0, keepdims=True)

    def masked(block):
        return jnp.concatenate([block * m for m in masks], axis=0)

    def pairs(tile):
        return dot_lanes(masked(flipped_x[:, lanes(tile)]), mixed[:, lanes(tile)])

    def near_only(step):
        tile = (1 - ctx) * half + step
        found = pairs(tile).astype(BF16)
        for q in range(per_tile):
            group = pl.ds(tile * per_tile + q, 1)
            part[0, group, :] = diagonals(found[q * rows : (q + 1) * rows] * upper)
            part[1, group, :] = jnp.zeros((1, rows), F32)

    def near_and_far(step):
        tile = ctx * half + step
        found = pairs(tile).astype(BF16)
        own_x, own_g, block = flipped_x[:, lanes(tile)], mixed[:, lanes(tile)], landed[:, lanes(tile)]
        across = dot_lanes(masked(jnp.where(first, own_x, block)), jnp.where(first, block, own_g)).astype(BF16)
        for q in range(per_tile):
            group = pl.ds(tile * per_tile + q, 1)
            inner, outer = found[q * rows : (q + 1) * rows], across[q * rows : (q + 1) * rows]
            part[0, group, :] = diagonals(inner * upper + outer * beyond)
            part[1, group, :] = diagonals(outer * upper)

    for tile in range(half):
        build(tile)
    for load in loads[1:]:
        load.wait()
    def prepare(at):
        flipped_x[:, at] = dot(backwards, conv_ref[:, at]).astype(BF16)
        mixed[:, at] = (gate_ref[:, at].astype(F32) * grad_ref[:, at].astype(F32)).astype(BF16)

    def columns(first_tile, count):
        return pl.ds(pl.multiple_of(first_tile * TILE, TILE), count * TILE)

    quarter = half // 2
    pieces = [
        columns((1 - ctx) * half, quarter),
        columns((1 - ctx) * half + quarter, quarter),
        columns(ctx * half, half),
    ]
    partner = {"ctx": 1 - ctx}

    def exchange(source, piece):
        return pltpu.make_async_remote_copy(
            src_ref=source.at[:, pieces[piece]], dst_ref=landed.at[:, pieces[piece]],
            send_sem=block_send.at[piece], recv_sem=block_recv.at[piece],
            device_id=partner, device_id_type=MESH,
        )

    def send(piece):
        @pl.when(ctx == 0)
        def _():
            exchange(flipped_x, piece).start()

        @pl.when(ctx == 1)
        def _():
            exchange(mixed, piece).start()

    prepare(columns((1 - ctx) * half, half))
    pl.semaphore_wait(barrier, peers - 1)
    send(0)
    send(1)
    prepare(columns(ctx * half, half))
    send(2)

    flipped[...] = dot(backwards, mixed[...]).astype(BF16)
    for step in range(half):
        near_only(step)

    first = ctx == 0
    for step in range(half):
        if step % quarter == 0:
            exchange(mixed, step // quarter).wait_recv()
        near_and_far(step)

    for peer in range(peers):
        h, e = peer // (rows // share), peer % (rows // share)
        tile8 = jnp.zeros((8, TILE), F32)
        for j in range(groups // 8):
            value = part[h, 8 * j : 8 * j + 8, :]
            shift = (share * (j - e) + 1) % TILE
            if shift:
                value = pltpu.roll(value, shift, 1)
            tile8 = jnp.where(lane // share == j, value, tile8)
        packed[peer] = tile8

    def send_sum(step):
        peer = lax.rem(me + step, peers)
        return pltpu.make_async_remote_copy(
            src_ref=packed.at[peer], dst_ref=arrived.at[step],
            send_sem=sum_send.at[step], recv_sem=sum_recv.at[step],
            device_id=place(peer), device_id_type=MESH,
        )

    copies = [send_sum(step) for step in range(1, peers)]
    for copy in copies:
        copy.start()

    exchange(mixed, 2).wait_recv()
    turned_block = dot(backwards, landed[...]).astype(BF16)
    zx[...] = jnp.where(first, jnp.zeros_like(turned_block), turned_block)
    zg[...] = jnp.where(first, turned_block, jnp.zeros_like(turned_block))

    def convolve(tile):
        at = lanes(tile)
        stacked = jnp.concatenate(
            [
                jnp.concatenate([conv_ref[:, at], flipped[:, at]], axis=1),
                jnp.concatenate([zx[:, at], zg[:, at]], axis=1),
            ],
            axis=0,
        )
        every = dot(mats[tile], stacked)
        total = every[:rows]
        for q in range(1, per_tile):
            total = jnp.where(both // size == q, every[q * rows : (q + 1) * rows], total)
        convolved = total[:, :TILE]
        out_ref[:, at] = (gate_ref[:, at].astype(F32) * convolved).astype(BF16)
        ggate_ref[:, at] = (grad_ref[:, at].astype(F32) * convolved).astype(BF16)
        turned_out[:, at] = total[:, TILE:].astype(BF16)

    saves = []
    for part_index in range(2):
        for tile in range(part_index * half, (part_index + 1) * half):
            if part_index == 0:
                build(tile + half)
            convolve(tile)
        at = slice(part_index * half * TILE, (part_index + 1) * half * TILE)
        gconv_ref[:, at] = dot(backwards, turned_out[:, at]).astype(BF16)

    for piece in range(3):
        exchange(mixed, piece).wait_send()
    summed = packed[me]
    for step, copy in zip(range(1, peers), copies):
        copy.wait()
        summed = summed + arrived[step]
    summed = summed * scale
    for j in range(groups // 8):
        value = summed if j == 0 else pltpu.roll(summed, TILE - share * j, 1)
        gkern_ref[8 * j : 8 * j + 8, :] = value[:, :share]
    for save in saves:
        save.wait()


def store_kernel(*refs):
    sems = refs[-1]
    copies = [pltpu.make_async_copy(refs[i], refs[4 + i], sems.at[i]) for i in range(4)]
    for copy in copies:
        copy.start()
    for copy in copies:
        copy.wait()


def fused_body(gate_input, conv_input, grad_output, kernel):
    _, rows, channels = conv_input.shape
    groups, lag_count = kernel.shape
    tiles = channels // TILE
    peers = lax.axis_size("dp") * lax.axis_size("ctx")
    scale = 1.0 / math.sqrt(lax.axis_size("dp") * rows * lax.axis_size("ctx"))
    block = jax.ShapeDtypeStruct((rows, channels), BF16)
    vmem = pl.BlockSpec(memory_space=pltpu.VMEM)
    hbm = pl.BlockSpec(memory_space=pltpu.HBM)
    results = pl.pallas_call(
        functools.partial(fused_kernel, peers, scale),
        out_shape=[block, block, block, jax.ShapeDtypeStruct((groups, lag_count // peers), F32)],
        in_specs=[hbm] * 4,
        out_specs=[vmem] * 4,
        scratch_shapes=[pltpu.VMEM((rows, channels), BF16)] * 3
        + [pltpu.VMEM((groups, lag_count), BF16)]
        + [pltpu.VMEM((rows, channels), BF16)] * 7
        + [
            pltpu.VMEM((2, groups, rows), F32),
            pltpu.VMEM((tiles, (groups // tiles) * rows, 2 * rows), BF16),
            pltpu.VMEM((2, groups, rows), F32),
            pltpu.VMEM((peers, 8, TILE), F32),
            pltpu.VMEM((peers, 8, TILE), F32),
            pltpu.SemaphoreType.DMA((4,)),
            pltpu.SemaphoreType.DMA((2, 3)),
            pltpu.SemaphoreType.DMA((3,)),
            pltpu.SemaphoreType.DMA((3,)),
            pltpu.SemaphoreType.DMA((peers,)),
            pltpu.SemaphoreType.DMA((peers,)),
        ],
        compiler_params=pltpu.CompilerParams(
            collective_id=0, has_side_effects=True, vmem_limit_bytes=VMEM_BYTES
        ),
        cost_estimate=pl.CostEstimate(
            flops=20 * rows * rows * channels, bytes_accessed=12 * rows * channels, transcendentals=0
        ),
    )(gate_input[0], conv_input[0], grad_output[0], kernel)
    results = pl.pallas_call(
        store_kernel,
        out_shape=[block, block, block, jax.ShapeDtypeStruct((groups, lag_count // peers), F32)],
        in_specs=[vmem] * 4,
        out_specs=[hbm] * 4,
        scratch_shapes=[pltpu.SemaphoreType.DMA((4,))],
        compiler_params=pltpu.CompilerParams(vmem_limit_bytes=VMEM_BYTES),
    )(*results)
    return (results[0][None], results[1][None], results[2][None], results[3])


def body(gate_input, conv_input, grad_output, kernel):
    _, rows, channels = conv_input.shape
    groups, lag_count = kernel.shape
    peers = lax.axis_size("dp") * lax.axis_size("ctx")
    fits = (
        lax.axis_size("ctx") == 2
        and rows == TILE
        and lag_count == 2 * rows
        and channels % (2 * TILE) == 0
        and TILE % (channels // groups) == 0
        and lag_count % peers == 0
        and rows % (lag_count // peers) == 0
        and groups * (lag_count // peers) == 8 * TILE
    )
    if fits:
        return fused_body(gate_input, conv_input, grad_output, kernel)
    return general_body(gate_input, conv_input, grad_output, kernel)


def solution(mesh):
    return jax.shard_map(
        body,
        mesh=mesh,
        in_specs=(P("dp", "ctx", "ch"), P("dp", "ctx", "ch"), P("dp", "ctx", "ch"), P("ch", None)),
        out_specs=(
            P("dp", "ctx", "ch"),
            P("dp", "ctx", "ch"),
            P("dp", "ctx", "ch"),
            P("ch", ("dp", "ctx")),
        ),
        check_vma=False,
    )
```

```python
import functools
import math

import jax
import jax.numpy as jnp
from jax import lax
from jax.experimental import pallas as pl
from jax.experimental.pallas import tpu as pltpu
from jax.sharding import PartitionSpec as P


def toeplitz(padded_kernel, offset, tok_rows):
    groups = padded_kernel.shape[0]
    segment = lax.dynamic_slice_in_dim(padded_kernel, offset * tok_rows + 1, 2 * tok_rows, 1)
    reverse = segment[:, ::-1]
    rolled = jnp.concatenate([reverse[:, tok_rows:], reverse[:, :tok_rows]], axis=1)
    tiled = jnp.tile(rolled, (1, tok_rows))[:, : tok_rows * (2 * tok_rows - 1)]
    return tiled.reshape(groups, tok_rows, 2 * tok_rows - 1)[:, :, :tok_rows]


def diagonal_sums(matrix):
    groups = matrix.shape[0]
    extent = matrix.shape[1]
    flipped = matrix[:, :, ::-1]
    padded = jnp.pad(flipped, ((0, 0), (0, 0), (0, extent)))
    flattened = padded.reshape(groups, 2 * extent * extent)[:, : extent * (2 * extent - 1)]
    totals = jnp.sum(flattened.reshape(groups, extent, 2 * extent - 1), axis=1, dtype=jnp.float32)
    return jnp.pad(totals, ((0, 0), (0, 1)))


def general_body(gate_input, conv_input, grad_output, kernel):
    tok_rows = gate_input.shape[1]
    channels = gate_input.shape[2]
    groups = kernel.shape[0]
    group_size = channels // groups
    lag_count = kernel.shape[1]
    lag_blocks = lag_count // tok_rows
    padded_kernel = jnp.pad(kernel, ((0, 0), (tok_rows, 2 * tok_rows)))
    blocks = lax.axis_size("ctx")
    own_block = lax.axis_index("ctx")
    gate_rows = gate_input[0]
    grad_rows = grad_output[0]
    grad_mixed = (gate_rows.astype(jnp.float32) * grad_rows.astype(jnp.float32)).astype(
        jnp.bfloat16
    )

    def forward_add(running, matrix, block):
        shaped = block.reshape(tok_rows, groups, group_size)
        return running + jnp.einsum(
            "gab,bgc->agc", matrix, shaped, preferred_element_type=jnp.float32
        ).reshape(tok_rows, channels)

    def backward_add(running, matrix, block):
        shaped = block.reshape(tok_rows, groups, group_size)
        return running + jnp.einsum(
            "gab,agc->bgc", matrix, shaped, preferred_element_type=jnp.float32
        ).reshape(tok_rows, channels)

    def window_add(buffer, grad_block, value_block, offset):
        left_side = grad_block.reshape(tok_rows, groups, group_size)
        right_side = value_block.reshape(tok_rows, groups, group_size)
        paired = jnp.einsum(
            "agc,bgc->gab", left_side, right_side, preferred_element_type=jnp.float32
        ).astype(jnp.bfloat16)
        window = diagonal_sums(paired)
        first_col = offset * tok_rows
        current = lax.dynamic_slice_in_dim(buffer, first_col, 2 * tok_rows, 1)
        return lax.dynamic_update_slice_in_dim(buffer, current + window, first_col, 1)

    def visit_block(carried, value_block, grad_block, offset, has_value, has_grad):
        convolved, grad_vals, buffer = carried
        bounded = jnp.minimum(offset, lag_blocks)
        matrix = toeplitz(padded_kernel, bounded, tok_rows)
        convolved = lax.cond(
            has_value, lambda: forward_add(convolved, matrix, value_block), lambda: convolved
        )
        grad_vals = lax.cond(
            has_grad, lambda: backward_add(grad_vals, matrix, grad_block), lambda: grad_vals
        )
        buffer = lax.cond(
            has_value, lambda: window_add(buffer, grad_mixed, value_block, bounded), lambda: buffer
        )
        return (convolved, grad_vals, buffer)

    initial = (
        jnp.zeros((tok_rows, channels), jnp.float32),
        jnp.zeros((tok_rows, channels), jnp.float32),
        jnp.zeros((groups, lag_count + 2 * tok_rows), jnp.float32),
    )
    value_shard = lax.all_gather(conv_input, "ctx", axis=1, tiled=True)
    grad_shard = lax.all_gather(grad_mixed[None], "ctx", axis=1, tiled=True)
    pieces = value_shard.shape[1] // tok_rows

    def per_block(position, carried_now):
        value_block = lax.dynamic_slice_in_dim(value_shard[0], position * tok_rows, tok_rows, 0)
        grad_block = lax.dynamic_slice_in_dim(grad_shard[0], position * tok_rows, tok_rows, 0)
        distance = jnp.abs(own_block - position)
        near = distance <= lag_blocks
        return visit_block(
            carried_now,
            value_block,
            grad_block,
            distance,
            (position <= own_block) & near,
            (position >= own_block) & near,
        )

    carried = lax.fori_loop(0, pieces, per_block, initial)
    convolved, grad_vals, buffer = carried
    output = (gate_rows.astype(jnp.float32) * convolved).astype(jnp.bfloat16)[None]
    grad_gate = (grad_rows.astype(jnp.float32) * convolved).astype(jnp.bfloat16)[None]
    grad_conv = grad_vals.astype(jnp.bfloat16)[None]
    partial_value = buffer[:, tok_rows - 1 : tok_rows - 1 + lag_count]
    summed = lax.psum_scatter(partial_value, ("dp", "ctx"), scatter_dimension=1, tiled=True)
    grad_kernel = summed / math.sqrt(lax.axis_size("dp") * tok_rows * blocks)
    return (output, grad_gate, grad_conv, grad_kernel)


TILE = 128
STRIP = 16
VMEM_BYTES = 53 * 1024 * 1024
F32, BF16 = jnp.float32, jnp.bfloat16
MESH = pl.DeviceIdType.MESH


def dot(left, right):
    return jnp.dot(left, right, preferred_element_type=F32)


def dot_lanes(left, right):
    return lax.dot_general(left, right, (((1,), (1,)), ((), ())), preferred_element_type=F32)


def iota(shape, dim):
    return lax.broadcasted_iota(jnp.int32, shape, dim)


def repeat(start, stop, step):
    def run(index, nothing):
        step(index)
        return nothing

    lax.fori_loop(start, stop, run, 0)


def fused_kernel(
    peers, scale,
    gate_hbm, conv_hbm, grad_hbm, taps_hbm,
    out_ref, ggate_ref, gconv_ref, gkern_ref,
    gate_ref, conv_ref, grad_ref, taps_ref, mixed, flipped, flipped_x, landed, zx, zg, turned_out, rev_taps, mats, part, packed, arrived,
    load_sem, save_sem, block_send, block_recv, sum_send, sum_recv,
):
    rows, channels = conv_ref.shape
    groups = taps_ref.shape[0]
    size = channels // groups
    per_tile = TILE // size
    tiles = channels // TILE
    half = tiles // 2
    dp, ctx = lax.axis_index("dp"), lax.axis_index("ctx")
    me = dp * 2 + ctx
    share = gkern_ref.shape[1]

    def place(index):
        return {"dp": index // 2, "ctx": lax.rem(index, 2)}

    loads = [
        pltpu.make_async_copy(source, target, load_sem.at[i])
        for i, (source, target) in enumerate(
            [(taps_hbm, taps_ref), (gate_hbm, gate_ref), (grad_hbm, grad_ref), (conv_hbm, conv_ref)]
        )
    ]
    for load in loads:
        load.start()

    barrier = pltpu.get_barrier_semaphore()
    for step in range(1, peers):
        pl.semaphore_signal(barrier, inc=1, device_id=place(lax.rem(me + step, peers)), device_id_type=MESH)

    row, col = iota((rows, rows), 0), iota((rows, rows), 1)
    upper = (row + col >= rows - 1).astype(F32).astype(BF16)
    beyond = (row + col < rows - 1).astype(F32).astype(BF16)
    backwards = jnp.where(row + col == rows - 1, 1.0, 0.0).astype(BF16)
    wrapped = jnp.where(lax.rem(row + col, rows) == 0, 1.0, 0.0).astype(BF16)
    loads[0].wait()
    rev_taps[0] = dot(taps_ref[:, :rows], wrapped)
    rev_taps[1] = dot(taps_ref[:, rows:], wrapped)

    lane = iota((1, TILE), 1)
    both = lax.rem(iota((1, 2 * TILE), 1), TILE)
    masks = [((lane // size) == q).astype(F32).astype(BF16) for q in range(per_tile)]

    def lanes(tile):
        start = tile * TILE
        return pl.ds(start if isinstance(tile, int) else pl.multiple_of(start, TILE), TILE)

    def bits(mask):
        return mask.astype(F32).astype(BF16)

    strips = rows // STRIP
    strip_row, strip_col = iota((STRIP, rows), 0), iota((STRIP, rows), 1)
    below = [bits(strip_row + n * STRIP >= strip_col) for n in range(strips)]
    above = [bits(strip_row + n * STRIP < strip_col) for n in range(strips)]

    def turn(strip, n):
        return pltpu.roll(strip, n * STRIP, 1) if n else strip

    def build(tile):
        for q in range(per_tile):
            group = pl.ds(tile * per_tile + q, 1)
            near, far = [
                pltpu.roll(
                    jnp.broadcast_to(rev_taps[h, group, :], (STRIP, rows)), 0, 1, stride=1, stride_axis=0
                ).astype(BF16)
                for h in range(2)
            ]
            for n in range(strips):
                at = slice(q * rows + n * STRIP, q * rows + (n + 1) * STRIP)
                near_n, far_n = turn(near, n), turn(far, n)
                mats[tile, at, :rows] = near_n * below[n]
                mats[tile, at, rows:] = far_n * below[n] + near_n * above[n]

    def diagonals(matrix):
        total = jnp.zeros((STRIP, rows), F32)
        for n in range(strips):
            total = total + turn(matrix[n * STRIP : (n + 1) * STRIP], n).astype(F32)
        turned = pltpu.roll(total, 0, 1, stride=1, stride_axis=0)
        return jnp.sum(turned, axis=0, keepdims=True)

    def masked(block):
        return jnp.concatenate([block * m for m in masks], axis=0)

    def pairs(tile):
        return dot_lanes(masked(flipped_x[:, lanes(tile)]), mixed[:, lanes(tile)])

    def near_only(step):
        tile = (1 - ctx) * half + step
        found = pairs(tile).astype(BF16)
        for q in range(per_tile):
            group = pl.ds(tile * per_tile + q, 1)
            part[0, group, :] = diagonals(found[q * rows : (q + 1) * rows] * upper)
            part[1, group, :] = jnp.zeros((1, rows), F32)

    def near_and_far(step):
        tile = ctx * half + step
        found = pairs(tile).astype(BF16)
        own_x, own_g, block = flipped_x[:, lanes(tile)], mixed[:, lanes(tile)], landed[:, lanes(tile)]
        across = dot_lanes(masked(jnp.where(first, own_x, block)), jnp.where(first, block, own_g)).astype(BF16)
        for q in range(per_tile):
            group = pl.ds(tile * per_tile + q, 1)
            inner, outer = found[q * rows : (q + 1) * rows], across[q * rows : (q + 1) * rows]
            part[0, group, :] = diagonals(inner * upper + outer * beyond)
            part[1, group, :] = diagonals(outer * upper)

    repeat(0, half, build)
    for load in loads[1:]:
        load.wait()
    def prepare(at):
        flipped_x[:, at] = dot(backwards, conv_ref[:, at]).astype(BF16)
        mixed[:, at] = (gate_ref[:, at].astype(F32) * grad_ref[:, at].astype(F32)).astype(BF16)

    def columns(first_tile, count):
        return pl.ds(pl.multiple_of(first_tile * TILE, TILE), count * TILE)

    quarter = half // 2
    pieces = [
        columns((1 - ctx) * half, quarter),
        columns((1 - ctx) * half + quarter, quarter),
        columns(ctx * half, half),
    ]
    partner = {"ctx": 1 - ctx}

    def exchange(source, piece):
        return pltpu.make_async_remote_copy(
            src_ref=source.at[:, pieces[piece]], dst_ref=landed.at[:, pieces[piece]],
            send_sem=block_send.at[piece], recv_sem=block_recv.at[piece],
            device_id=partner, device_id_type=MESH,
        )

    def send(piece):
        @pl.when(ctx == 0)
        def _():
            exchange(flipped_x, piece).start()

        @pl.when(ctx == 1)
        def _():
            exchange(mixed, piece).start()

    prepare(columns((1 - ctx) * half, half))
    pl.semaphore_wait(barrier, peers - 1)
    send(0)
    send(1)
    prepare(columns(ctx * half, half))
    send(2)

    flipped[...] = dot(backwards, mixed[...]).astype(BF16)
    repeat(0, half, near_only)

    first = ctx == 0
    for piece in range(2):
        exchange(mixed, piece).wait_recv()
        repeat(piece * quarter, (piece + 1) * quarter, near_and_far)

    for peer in range(peers):
        h, e = peer // (rows // share), peer % (rows // share)
        tile8 = jnp.zeros((8, TILE), F32)
        for j in range(groups // 8):
            value = part[h, 8 * j : 8 * j + 8, :]
            shift = (share * (j - e) + 1) % TILE
            if shift:
                value = pltpu.roll(value, shift, 1)
            tile8 = jnp.where(lane // share == j, value, tile8)
        packed[peer] = tile8

    def send_sum(step):
        peer = lax.rem(me + step, peers)
        return pltpu.make_async_remote_copy(
            src_ref=packed.at[peer], dst_ref=arrived.at[step],
            send_sem=sum_send.at[step], recv_sem=sum_recv.at[step],
            device_id=place(peer), device_id_type=MESH,
        )

    copies = [send_sum(step) for step in range(1, peers)]
    for copy in copies:
        copy.start()

    exchange(mixed, 2).wait_recv()
    turned_block = dot(backwards, landed[...]).astype(BF16)
    zx[...] = jnp.where(first, jnp.zeros_like(turned_block), turned_block)
    zg[...] = jnp.where(first, turned_block, jnp.zeros_like(turned_block))

    repeat(half, tiles, build)

    def convolve(tile):
        at = lanes(tile)
        stacked = jnp.concatenate(
            [
                jnp.concatenate([conv_ref[:, at], flipped[:, at]], axis=1),
                jnp.concatenate([zx[:, at], zg[:, at]], axis=1),
            ],
            axis=0,
        )
        every = dot(mats[tile], stacked)
        total = every[:rows]
        for q in range(1, per_tile):
            total = jnp.where(both // size == q, every[q * rows : (q + 1) * rows], total)
        convolved = total[:, :TILE]
        out_ref[:, at] = (gate_ref[:, at].astype(F32) * convolved).astype(BF16)
        ggate_ref[:, at] = (grad_ref[:, at].astype(F32) * convolved).astype(BF16)
        turned_out[:, at] = total[:, TILE:].astype(BF16)

    saves = []
    for part_index in range(2):
        repeat(part_index * half, (part_index + 1) * half, convolve)
        at = slice(part_index * half * TILE, (part_index + 1) * half * TILE)
        gconv_ref[:, at] = dot(backwards, turned_out[:, at]).astype(BF16)

    for piece in range(3):
        exchange(mixed, piece).wait_send()
    summed = packed[me]
    for step, copy in zip(range(1, peers), copies):
        copy.wait()
        summed = summed + arrived[step]
    summed = summed * scale
    for j in range(groups // 8):
        value = summed if j == 0 else pltpu.roll(summed, TILE - share * j, 1)
        gkern_ref[8 * j : 8 * j + 8, :] = value[:, :share]
    for save in saves:
        save.wait()


def store_kernel(*refs):
    sems = refs[-1]
    copies = [pltpu.make_async_copy(refs[i], refs[4 + i], sems.at[i]) for i in range(4)]
    for copy in copies:
        copy.start()
    for copy in copies:
        copy.wait()


def fused_body(gate_input, conv_input, grad_output, kernel):
    _, rows, channels = conv_input.shape
    groups, lag_count = kernel.shape
    tiles = channels // TILE
    peers = lax.axis_size("dp") * lax.axis_size("ctx")
    scale = 1.0 / math.sqrt(lax.axis_size("dp") * rows * lax.axis_size("ctx"))
    block = jax.ShapeDtypeStruct((rows, channels), BF16)
    vmem = pl.BlockSpec(memory_space=pltpu.VMEM)
    hbm = pl.BlockSpec(memory_space=pltpu.HBM)
    results = pl.pallas_call(
        functools.partial(fused_kernel, peers, scale),
        out_shape=[block, block, block, jax.ShapeDtypeStruct((groups, lag_count // peers), F32)],
        in_specs=[hbm] * 4,
        out_specs=[vmem] * 4,
        scratch_shapes=[pltpu.VMEM((rows, channels), BF16)] * 3
        + [pltpu.VMEM((groups, lag_count), BF16)]
        + [pltpu.VMEM((rows, channels), BF16)] * 7
        + [
            pltpu.VMEM((2, groups, rows), F32),
            pltpu.VMEM((tiles, (groups // tiles) * rows, 2 * rows), BF16),
            pltpu.VMEM((2, groups, rows), F32),
            pltpu.VMEM((peers, 8, TILE), F32),
            pltpu.VMEM((peers, 8, TILE), F32),
            pltpu.SemaphoreType.DMA((4,)),
            pltpu.SemaphoreType.DMA((2, 3)),
            pltpu.SemaphoreType.DMA((3,)),
            pltpu.SemaphoreType.DMA((3,)),
            pltpu.SemaphoreType.DMA((peers,)),
            pltpu.SemaphoreType.DMA((peers,)),
        ],
        compiler_params=pltpu.CompilerParams(
            collective_id=0, has_side_effects=True, vmem_limit_bytes=VMEM_BYTES
        ),
        cost_estimate=pl.CostEstimate(
            flops=20 * rows * rows * channels, bytes_accessed=12 * rows * channels, transcendentals=0
        ),
    )(gate_input[0], conv_input[0], grad_output[0], kernel)
    results = pl.pallas_call(
        store_kernel,
        out_shape=[block, block, block, jax.ShapeDtypeStruct((groups, lag_count // peers), F32)],
        in_specs=[vmem] * 4,
        out_specs=[hbm] * 4,
        scratch_shapes=[pltpu.SemaphoreType.DMA((4,))],
        compiler_params=pltpu.CompilerParams(vmem_limit_bytes=VMEM_BYTES),
    )(*results)
    return (results[0][None], results[1][None], results[2][None], results[3])


def body(gate_input, conv_input, grad_output, kernel):
    _, rows, channels = conv_input.shape
    groups, lag_count = kernel.shape
    peers = lax.axis_size("dp") * lax.axis_size("ctx")
    fits = (
        lax.axis_size("ctx") == 2
        and rows == TILE
        and lag_count == 2 * rows
        and channels % (2 * TILE) == 0
        and TILE % (channels // groups) == 0
        and lag_count % peers == 0
        and rows % (lag_count // peers) == 0
        and groups * (lag_count // peers) == 8 * TILE
    )
    if fits:
        return fused_body(gate_input, conv_input, grad_output, kernel)
    return general_body(gate_input, conv_input, grad_output, kernel)


def solution(mesh):
    return jax.shard_map(
        body,
        mesh=mesh,
        in_specs=(P("dp", "ctx", "ch"), P("dp", "ctx", "ch"), P("dp", "ctx", "ch"), P("ch", None)),
        out_specs=(
            P("dp", "ctx", "ch"),
            P("dp", "ctx", "ch"),
            P("dp", "ctx", "ch"),
            P("ch", ("dp", "ctx")),
        ),
        check_vma=False,
    )
```

```python
import functools
import math

import jax
import jax.numpy as jnp
from jax import lax
from jax.experimental import pallas as pl
from jax.experimental.pallas import tpu as pltpu
from jax.sharding import PartitionSpec as P


def toeplitz(padded_kernel, offset, tok_rows):
    groups = padded_kernel.shape[0]
    segment = lax.dynamic_slice_in_dim(padded_kernel, offset * tok_rows + 1, 2 * tok_rows, 1)
    reverse = segment[:, ::-1]
    rolled = jnp.concatenate([reverse[:, tok_rows:], reverse[:, :tok_rows]], axis=1)
    tiled = jnp.tile(rolled, (1, tok_rows))[:, : tok_rows * (2 * tok_rows - 1)]
    return tiled.reshape(groups, tok_rows, 2 * tok_rows - 1)[:, :, :tok_rows]


def diagonal_sums(matrix):
    groups = matrix.shape[0]
    extent = matrix.shape[1]
    flipped = matrix[:, :, ::-1]
    padded = jnp.pad(flipped, ((0, 0), (0, 0), (0, extent)))
    flattened = padded.reshape(groups, 2 * extent * extent)[:, : extent * (2 * extent - 1)]
    totals = jnp.sum(flattened.reshape(groups, extent, 2 * extent - 1), axis=1, dtype=jnp.float32)
    return jnp.pad(totals, ((0, 0), (0, 1)))


def general_body(gate_input, conv_input, grad_output, kernel):
    tok_rows = gate_input.shape[1]
    channels = gate_input.shape[2]
    groups = kernel.shape[0]
    group_size = channels // groups
    lag_count = kernel.shape[1]
    lag_blocks = lag_count // tok_rows
    padded_kernel = jnp.pad(kernel, ((0, 0), (tok_rows, 2 * tok_rows)))
    blocks = lax.axis_size("ctx")
    own_block = lax.axis_index("ctx")
    gate_rows = gate_input[0]
    grad_rows = grad_output[0]
    grad_mixed = (gate_rows.astype(jnp.float32) * grad_rows.astype(jnp.float32)).astype(
        jnp.bfloat16
    )

    def forward_add(running, matrix, block):
        shaped = block.reshape(tok_rows, groups, group_size)
        return running + jnp.einsum(
            "gab,bgc->agc", matrix, shaped, preferred_element_type=jnp.float32
        ).reshape(tok_rows, channels)

    def backward_add(running, matrix, block):
        shaped = block.reshape(tok_rows, groups, group_size)
        return running + jnp.einsum(
            "gab,agc->bgc", matrix, shaped, preferred_element_type=jnp.float32
        ).reshape(tok_rows, channels)

    def window_add(buffer, grad_block, value_block, offset):
        left_side = grad_block.reshape(tok_rows, groups, group_size)
        right_side = value_block.reshape(tok_rows, groups, group_size)
        paired = jnp.einsum(
            "agc,bgc->gab", left_side, right_side, preferred_element_type=jnp.float32
        ).astype(jnp.bfloat16)
        window = diagonal_sums(paired)
        first_col = offset * tok_rows
        current = lax.dynamic_slice_in_dim(buffer, first_col, 2 * tok_rows, 1)
        return lax.dynamic_update_slice_in_dim(buffer, current + window, first_col, 1)

    def visit_block(carried, value_block, grad_block, offset, has_value, has_grad):
        convolved, grad_vals, buffer = carried
        bounded = jnp.minimum(offset, lag_blocks)
        matrix = toeplitz(padded_kernel, bounded, tok_rows)
        convolved = lax.cond(
            has_value, lambda: forward_add(convolved, matrix, value_block), lambda: convolved
        )
        grad_vals = lax.cond(
            has_grad, lambda: backward_add(grad_vals, matrix, grad_block), lambda: grad_vals
        )
        buffer = lax.cond(
            has_value, lambda: window_add(buffer, grad_mixed, value_block, bounded), lambda: buffer
        )
        return (convolved, grad_vals, buffer)

    initial = (
        jnp.zeros((tok_rows, channels), jnp.float32),
        jnp.zeros((tok_rows, channels), jnp.float32),
        jnp.zeros((groups, lag_count + 2 * tok_rows), jnp.float32),
    )
    value_shard = lax.all_gather(conv_input, "ctx", axis=1, tiled=True)
    grad_shard = lax.all_gather(grad_mixed[None], "ctx", axis=1, tiled=True)
    pieces = value_shard.shape[1] // tok_rows

    def per_block(position, carried_now):
        value_block = lax.dynamic_slice_in_dim(value_shard[0], position * tok_rows, tok_rows, 0)
        grad_block = lax.dynamic_slice_in_dim(grad_shard[0], position * tok_rows, tok_rows, 0)
        distance = jnp.abs(own_block - position)
        near = distance <= lag_blocks
        return visit_block(
            carried_now,
            value_block,
            grad_block,
            distance,
            (position <= own_block) & near,
            (position >= own_block) & near,
        )

    carried = lax.fori_loop(0, pieces, per_block, initial)
    convolved, grad_vals, buffer = carried
    output = (gate_rows.astype(jnp.float32) * convolved).astype(jnp.bfloat16)[None]
    grad_gate = (grad_rows.astype(jnp.float32) * convolved).astype(jnp.bfloat16)[None]
    grad_conv = grad_vals.astype(jnp.bfloat16)[None]
    partial_value = buffer[:, tok_rows - 1 : tok_rows - 1 + lag_count]
    summed = lax.psum_scatter(partial_value, ("dp", "ctx"), scatter_dimension=1, tiled=True)
    grad_kernel = summed / math.sqrt(lax.axis_size("dp") * tok_rows * blocks)
    return (output, grad_gate, grad_conv, grad_kernel)


TILE = 128
STRIP = 16
VMEM_BYTES = 53 * 1024 * 1024
F32, BF16 = jnp.float32, jnp.bfloat16
MESH = pl.DeviceIdType.MESH


def dot(left, right):
    return jnp.dot(left, right, preferred_element_type=F32)


def dot_lanes(left, right):
    return lax.dot_general(left, right, (((1,), (1,)), ((), ())), preferred_element_type=F32)


def iota(shape, dim):
    return lax.broadcasted_iota(jnp.int32, shape, dim)


def fused_kernel(
    peers, scale,
    gate_hbm, conv_hbm, grad_hbm, taps_hbm,
    out_ref, ggate_ref, gconv_ref, gkern_ref,
    gate_ref, conv_ref, grad_ref, taps_ref, mixed, flipped, flipped_x, landed, early_in, zx, zg, turned_out, rev_taps, mats, part, packed, arrived,
    load_sem, early_send, early_recv, save_sem, block_send, block_recv, sum_send, sum_recv,
):
    rows, channels = conv_ref.shape
    groups = taps_ref.shape[0]
    size = channels // groups
    per_tile = TILE // size
    tiles = channels // TILE
    half = tiles // 2
    dp, ctx = lax.axis_index("dp"), lax.axis_index("ctx")
    me = dp * 2 + ctx
    share = gkern_ref.shape[1]

    def place(index):
        return {"dp": index // 2, "ctx": lax.rem(index, 2)}

    loads = [
        pltpu.make_async_copy(source, target, load_sem.at[i])
        for i, (source, target) in enumerate(
            [(taps_hbm, taps_ref), (gate_hbm, gate_ref), (grad_hbm, grad_ref), (conv_hbm, conv_ref)]
        )
    ]
    for load in loads:
        load.start()

    barrier = pltpu.get_barrier_semaphore()
    for step in range(1, peers):
        pl.semaphore_signal(barrier, inc=1, device_id=place(lax.rem(me + step, peers)), device_id_type=MESH)

    def columns(first_tile, count):
        return pl.ds(pl.multiple_of(first_tile * TILE, TILE), count * TILE)

    partner = {"ctx": 1 - ctx}

    def early(source, slot):
        return pltpu.make_async_remote_copy(
            src_ref=source.at[:, columns((1 - ctx) * half, half)], dst_ref=early_in.at[slot],
            send_sem=early_send.at[slot], recv_sem=early_recv.at[slot],
            device_id=partner, device_id_type=MESH,
        )

    pl.semaphore_wait(barrier, peers - 1)

    @pl.when(ctx == 0)
    def _():
        early(conv_hbm, 0).start()

    @pl.when(ctx == 1)
    def _():
        early(gate_hbm, 0).start()
        early(grad_hbm, 1).start()

    row, col = iota((rows, rows), 0), iota((rows, rows), 1)
    upper = (row + col >= rows - 1).astype(F32).astype(BF16)
    beyond = (row + col < rows - 1).astype(F32).astype(BF16)
    backwards = jnp.where(row + col == rows - 1, 1.0, 0.0).astype(BF16)
    wrapped = jnp.where(lax.rem(row + col, rows) == 0, 1.0, 0.0).astype(BF16)
    loads[0].wait()
    rev_taps[0] = dot(taps_ref[:, :rows], wrapped)
    rev_taps[1] = dot(taps_ref[:, rows:], wrapped)

    lane = iota((1, TILE), 1)
    both = lax.rem(iota((1, 2 * TILE), 1), TILE)
    masks = [((lane // size) == q).astype(F32).astype(BF16) for q in range(per_tile)]

    def lanes(tile):
        start = tile * TILE
        return pl.ds(start if isinstance(tile, int) else pl.multiple_of(start, TILE), TILE)

    def bits(mask):
        return mask.astype(F32).astype(BF16)

    strips = rows // STRIP
    strip_row, strip_col = iota((STRIP, rows), 0), iota((STRIP, rows), 1)
    below = [bits(strip_row + n * STRIP >= strip_col) for n in range(strips)]
    above = [bits(strip_row + n * STRIP < strip_col) for n in range(strips)]

    def turn(strip, n):
        return pltpu.roll(strip, n * STRIP, 1) if n else strip

    def build(tile):
        for q in range(per_tile):
            group = pl.ds(tile * per_tile + q, 1)
            near, far = [
                pltpu.roll(
                    jnp.broadcast_to(rev_taps[h, group, :], (STRIP, rows)), 0, 1, stride=1, stride_axis=0
                ).astype(BF16)
                for h in range(2)
            ]
            for n in range(strips):
                at = slice(q * rows + n * STRIP, q * rows + (n + 1) * STRIP)
                near_n, far_n = turn(near, n), turn(far, n)
                mats[tile, at, :rows] = near_n * below[n]
                mats[tile, at, rows:] = far_n * below[n] + near_n * above[n]

    def diagonals(matrix):
        total = jnp.zeros((STRIP, rows), F32)
        for n in range(strips):
            total = total + turn(matrix[n * STRIP : (n + 1) * STRIP], n).astype(F32)
        turned = pltpu.roll(total, 0, 1, stride=1, stride_axis=0)
        return jnp.sum(turned, axis=0, keepdims=True)

    def masked(block):
        return jnp.concatenate([block * m for m in masks], axis=0)

    def pairs(tile):
        return dot_lanes(masked(flipped_x[:, lanes(tile)]), mixed[:, lanes(tile)])

    def near_only(step):
        tile = (1 - ctx) * half + step
        found = pairs(tile).astype(BF16)
        for q in range(per_tile):
            group = pl.ds(tile * per_tile + q, 1)
            part[0, group, :] = diagonals(found[q * rows : (q + 1) * rows] * upper)
            part[1, group, :] = jnp.zeros((1, rows), F32)

    def near_and_far(step):
        tile = ctx * half + step
        found = pairs(tile).astype(BF16)
        own_x, own_g, block = flipped_x[:, lanes(tile)], mixed[:, lanes(tile)], landed[:, lanes(tile)]
        across = dot_lanes(masked(jnp.where(first, own_x, block)), jnp.where(first, block, own_g)).astype(BF16)
        for q in range(per_tile):
            group = pl.ds(tile * per_tile + q, 1)
            inner, outer = found[q * rows : (q + 1) * rows], across[q * rows : (q + 1) * rows]
            part[0, group, :] = diagonals(inner * upper + outer * beyond)
            part[1, group, :] = diagonals(outer * upper)

    for tile in range(half):
        build(tile)
    for load in loads[1:]:
        load.wait()
    def prepare(at):
        flipped_x[:, at] = dot(backwards, conv_ref[:, at]).astype(BF16)
        mixed[:, at] = (gate_ref[:, at].astype(F32) * grad_ref[:, at].astype(F32)).astype(BF16)

    rest = columns(ctx * half, half)

    def exchange(source):
        return pltpu.make_async_remote_copy(
            src_ref=source.at[:, rest], dst_ref=landed.at[:, rest],
            send_sem=block_send, recv_sem=block_recv,
            device_id=partner, device_id_type=MESH,
        )

    prepare(slice(None))

    @pl.when(ctx == 0)
    def _():
        exchange(flipped_x).start()

    @pl.when(ctx == 1)
    def _():
        exchange(mixed).start()

    for step in range(half):
        near_only(step)

    first = ctx == 0

    @pl.when(ctx == 0)
    def _():
        early(gate_hbm, 0).wait_recv()
        early(grad_hbm, 1).wait_recv()
        landed[:, : half * TILE] = (early_in[0].astype(F32) * early_in[1].astype(F32)).astype(BF16)

    @pl.when(ctx == 1)
    def _():
        early(conv_hbm, 0).wait_recv()
        landed[:, half * TILE :] = dot(backwards, early_in[0]).astype(BF16)

    for step in range(half):
        near_and_far(step)

    for peer in range(peers):
        h, e = peer // (rows // share), peer % (rows // share)
        tile8 = jnp.zeros((8, TILE), F32)
        for j in range(groups // 8):
            value = part[h, 8 * j : 8 * j + 8, :]
            shift = (share * (j - e) + 1) % TILE
            if shift:
                value = pltpu.roll(value, shift, 1)
            tile8 = jnp.where(lane // share == j, value, tile8)
        packed[peer] = tile8

    def send_sum(step):
        peer = lax.rem(me + step, peers)
        return pltpu.make_async_remote_copy(
            src_ref=packed.at[peer], dst_ref=arrived.at[step],
            send_sem=sum_send.at[step], recv_sem=sum_recv.at[step],
            device_id=place(peer), device_id_type=MESH,
        )

    copies = [send_sum(step) for step in range(1, peers)]
    for copy in copies:
        copy.start()

    flipped[...] = dot(backwards, mixed[...]).astype(BF16)
    exchange(mixed).wait_recv()
    turned_block = dot(backwards, landed[...]).astype(BF16)
    zx[...] = jnp.where(first, jnp.zeros_like(turned_block), turned_block)
    zg[...] = jnp.where(first, turned_block, jnp.zeros_like(turned_block))

    def convolve(tile):
        at = lanes(tile)
        stacked = jnp.concatenate(
            [
                jnp.concatenate([conv_ref[:, at], flipped[:, at]], axis=1),
                jnp.concatenate([zx[:, at], zg[:, at]], axis=1),
            ],
            axis=0,
        )
        every = dot(mats[tile], stacked)
        total = every[:rows]
        for q in range(1, per_tile):
            total = jnp.where(both // size == q, every[q * rows : (q + 1) * rows], total)
        convolved = total[:, :TILE]
        out_ref[:, at] = (gate_ref[:, at].astype(F32) * convolved).astype(BF16)
        ggate_ref[:, at] = (grad_ref[:, at].astype(F32) * convolved).astype(BF16)
        turned_out[:, at] = total[:, TILE:].astype(BF16)

    saves = []
    for part_index in range(2):
        for tile in range(part_index * half, (part_index + 1) * half):
            if part_index == 0:
                build(tile + half)
            convolve(tile)
        at = slice(part_index * half * TILE, (part_index + 1) * half * TILE)
        gconv_ref[:, at] = dot(backwards, turned_out[:, at]).astype(BF16)

    exchange(mixed).wait_send()

    @pl.when(ctx == 0)
    def _():
        early(conv_hbm, 0).wait_send()

    @pl.when(ctx == 1)
    def _():
        early(gate_hbm, 0).wait_send()
        early(grad_hbm, 1).wait_send()

    summed = packed[me]
    for step, copy in zip(range(1, peers), copies):
        copy.wait()
        summed = summed + arrived[step]
    summed = summed * scale
    for j in range(groups // 8):
        value = summed if j == 0 else pltpu.roll(summed, TILE - share * j, 1)
        gkern_ref[8 * j : 8 * j + 8, :] = value[:, :share]
    for save in saves:
        save.wait()


def store_kernel(*refs):
    sems = refs[-1]
    copies = [pltpu.make_async_copy(refs[i], refs[4 + i], sems.at[i]) for i in range(4)]
    for copy in copies:
        copy.start()
    for copy in copies:
        copy.wait()


def fused_body(gate_input, conv_input, grad_output, kernel):
    _, rows, channels = conv_input.shape
    groups, lag_count = kernel.shape
    tiles = channels // TILE
    peers = lax.axis_size("dp") * lax.axis_size("ctx")
    scale = 1.0 / math.sqrt(lax.axis_size("dp") * rows * lax.axis_size("ctx"))
    block = jax.ShapeDtypeStruct((rows, channels), BF16)
    vmem = pl.BlockSpec(memory_space=pltpu.VMEM)
    hbm = pl.BlockSpec(memory_space=pltpu.HBM)
    results = pl.pallas_call(
        functools.partial(fused_kernel, peers, scale),
        out_shape=[block, block, block, jax.ShapeDtypeStruct((groups, lag_count // peers), F32)],
        in_specs=[hbm] * 4,
        out_specs=[vmem] * 4,
        scratch_shapes=[pltpu.VMEM((rows, channels), BF16)] * 3
        + [pltpu.VMEM((groups, lag_count), BF16)]
        + [pltpu.VMEM((rows, channels), BF16)] * 4
        + [pltpu.VMEM((2, rows, channels // 2), BF16)]
        + [pltpu.VMEM((rows, channels), BF16)] * 3
        + [
            pltpu.VMEM((2, groups, rows), F32),
            pltpu.VMEM((tiles, (groups // tiles) * rows, 2 * rows), BF16),
            pltpu.VMEM((2, groups, rows), F32),
            pltpu.VMEM((peers, 8, TILE), F32),
            pltpu.VMEM((peers, 8, TILE), F32),
            pltpu.SemaphoreType.DMA((4,)),
            pltpu.SemaphoreType.DMA((2,)),
            pltpu.SemaphoreType.DMA((2,)),
            pltpu.SemaphoreType.DMA((2, 3)),
            pltpu.SemaphoreType.DMA,
            pltpu.SemaphoreType.DMA,
            pltpu.SemaphoreType.DMA((peers,)),
            pltpu.SemaphoreType.DMA((peers,)),
        ],
        compiler_params=pltpu.CompilerParams(
            collective_id=0, has_side_effects=True, vmem_limit_bytes=VMEM_BYTES
        ),
        cost_estimate=pl.CostEstimate(
            flops=20 * rows * rows * channels, bytes_accessed=12 * rows * channels, transcendentals=0
        ),
    )(gate_input[0], conv_input[0], grad_output[0], kernel)
    results = pl.pallas_call(
        store_kernel,
        out_shape=[block, block, block, jax.ShapeDtypeStruct((groups, lag_count // peers), F32)],
        in_specs=[vmem] * 4,
        out_specs=[hbm] * 4,
        scratch_shapes=[pltpu.SemaphoreType.DMA((4,))],
        compiler_params=pltpu.CompilerParams(vmem_limit_bytes=VMEM_BYTES),
    )(*results)
    return (results[0][None], results[1][None], results[2][None], results[3])


def body(gate_input, conv_input, grad_output, kernel):
    _, rows, channels = conv_input.shape
    groups, lag_count = kernel.shape
    peers = lax.axis_size("dp") * lax.axis_size("ctx")
    fits = (
        lax.axis_size("ctx") == 2
        and rows == TILE
        and lag_count == 2 * rows
        and channels % (2 * TILE) == 0
        and TILE % (channels // groups) == 0
        and lag_count % peers == 0
        and rows % (lag_count // peers) == 0
        and groups * (lag_count // peers) == 8 * TILE
    )
    if fits:
        return fused_body(gate_input, conv_input, grad_output, kernel)
    return general_body(gate_input, conv_input, grad_output, kernel)


def solution(mesh):
    return jax.shard_map(
        body,
        mesh=mesh,
        in_specs=(P("dp", "ctx", "ch"), P("dp", "ctx", "ch"), P("dp", "ctx", "ch"), P("ch", None)),
        out_specs=(
            P("dp", "ctx", "ch"),
            P("dp", "ctx", "ch"),
            P("dp", "ctx", "ch"),
            P("ch", ("dp", "ctx")),
        ),
        check_vma=False,
    )
```

```python
import functools
import math

import jax
import jax.numpy as jnp
from jax import lax
from jax.experimental import pallas as pl
from jax.experimental.pallas import tpu as pltpu
from jax.sharding import PartitionSpec as P


def toeplitz(padded_kernel, offset, tok_rows):
    groups = padded_kernel.shape[0]
    segment = lax.dynamic_slice_in_dim(padded_kernel, offset * tok_rows + 1, 2 * tok_rows, 1)
    reverse = segment[:, ::-1]
    rolled = jnp.concatenate([reverse[:, tok_rows:], reverse[:, :tok_rows]], axis=1)
    tiled = jnp.tile(rolled, (1, tok_rows))[:, : tok_rows * (2 * tok_rows - 1)]
    return tiled.reshape(groups, tok_rows, 2 * tok_rows - 1)[:, :, :tok_rows]


def diagonal_sums(matrix):
    groups = matrix.shape[0]
    extent = matrix.shape[1]
    flipped = matrix[:, :, ::-1]
    padded = jnp.pad(flipped, ((0, 0), (0, 0), (0, extent)))
    flattened = padded.reshape(groups, 2 * extent * extent)[:, : extent * (2 * extent - 1)]
    totals = jnp.sum(flattened.reshape(groups, extent, 2 * extent - 1), axis=1, dtype=jnp.float32)
    return jnp.pad(totals, ((0, 0), (0, 1)))


def general_body(gate_input, conv_input, grad_output, kernel):
    tok_rows = gate_input.shape[1]
    channels = gate_input.shape[2]
    groups = kernel.shape[0]
    group_size = channels // groups
    lag_count = kernel.shape[1]
    lag_blocks = lag_count // tok_rows
    padded_kernel = jnp.pad(kernel, ((0, 0), (tok_rows, 2 * tok_rows)))
    blocks = lax.axis_size("ctx")
    own_block = lax.axis_index("ctx")
    gate_rows = gate_input[0]
    grad_rows = grad_output[0]
    grad_mixed = (gate_rows.astype(jnp.float32) * grad_rows.astype(jnp.float32)).astype(
        jnp.bfloat16
    )

    def forward_add(running, matrix, block):
        shaped = block.reshape(tok_rows, groups, group_size)
        return running + jnp.einsum(
            "gab,bgc->agc", matrix, shaped, preferred_element_type=jnp.float32
        ).reshape(tok_rows, channels)

    def backward_add(running, matrix, block):
        shaped = block.reshape(tok_rows, groups, group_size)
        return running + jnp.einsum(
            "gab,agc->bgc", matrix, shaped, preferred_element_type=jnp.float32
        ).reshape(tok_rows, channels)

    def window_add(buffer, grad_block, value_block, offset):
        left_side = grad_block.reshape(tok_rows, groups, group_size)
        right_side = value_block.reshape(tok_rows, groups, group_size)
        paired = jnp.einsum(
            "agc,bgc->gab", left_side, right_side, preferred_element_type=jnp.float32
        ).astype(jnp.bfloat16)
        window = diagonal_sums(paired)
        first_col = offset * tok_rows
        current = lax.dynamic_slice_in_dim(buffer, first_col, 2 * tok_rows, 1)
        return lax.dynamic_update_slice_in_dim(buffer, current + window, first_col, 1)

    def visit_block(carried, value_block, grad_block, offset, has_value, has_grad):
        convolved, grad_vals, buffer = carried
        bounded = jnp.minimum(offset, lag_blocks)
        matrix = toeplitz(padded_kernel, bounded, tok_rows)
        convolved = lax.cond(
            has_value, lambda: forward_add(convolved, matrix, value_block), lambda: convolved
        )
        grad_vals = lax.cond(
            has_grad, lambda: backward_add(grad_vals, matrix, grad_block), lambda: grad_vals
        )
        buffer = lax.cond(
            has_value, lambda: window_add(buffer, grad_mixed, value_block, bounded), lambda: buffer
        )
        return (convolved, grad_vals, buffer)

    initial = (
        jnp.zeros((tok_rows, channels), jnp.float32),
        jnp.zeros((tok_rows, channels), jnp.float32),
        jnp.zeros((groups, lag_count + 2 * tok_rows), jnp.float32),
    )
    value_shard = lax.all_gather(conv_input, "ctx", axis=1, tiled=True)
    grad_shard = lax.all_gather(grad_mixed[None], "ctx", axis=1, tiled=True)
    pieces = value_shard.shape[1] // tok_rows

    def per_block(position, carried_now):
        value_block = lax.dynamic_slice_in_dim(value_shard[0], position * tok_rows, tok_rows, 0)
        grad_block = lax.dynamic_slice_in_dim(grad_shard[0], position * tok_rows, tok_rows, 0)
        distance = jnp.abs(own_block - position)
        near = distance <= lag_blocks
        return visit_block(
            carried_now,
            value_block,
            grad_block,
            distance,
            (position <= own_block) & near,
            (position >= own_block) & near,
        )

    carried = lax.fori_loop(0, pieces, per_block, initial)
    convolved, grad_vals, buffer = carried
    output = (gate_rows.astype(jnp.float32) * convolved).astype(jnp.bfloat16)[None]
    grad_gate = (grad_rows.astype(jnp.float32) * convolved).astype(jnp.bfloat16)[None]
    grad_conv = grad_vals.astype(jnp.bfloat16)[None]
    partial_value = buffer[:, tok_rows - 1 : tok_rows - 1 + lag_count]
    summed = lax.psum_scatter(partial_value, ("dp", "ctx"), scatter_dimension=1, tiled=True)
    grad_kernel = summed / math.sqrt(lax.axis_size("dp") * tok_rows * blocks)
    return (output, grad_gate, grad_conv, grad_kernel)


TILE = 128
STRIP = 16
VMEM_BYTES = 53 * 1024 * 1024
F32, BF16 = jnp.float32, jnp.bfloat16
MESH = pl.DeviceIdType.MESH


def dot(left, right):
    return jnp.dot(left, right, preferred_element_type=F32)


def dot_lanes(left, right):
    return lax.dot_general(left, right, (((1,), (1,)), ((), ())), preferred_element_type=F32)


def iota(shape, dim):
    return lax.broadcasted_iota(jnp.int32, shape, dim)


def fused_kernel(
    peers, scale,
    gate_hbm, conv_hbm, grad_hbm, taps_hbm,
    out_ref, ggate_ref, gconv_ref, gkern_ref,
    gate_ref, conv_ref, grad_ref, taps_ref, mixed, flipped, flipped_x, landed, early_in, zx, zg, turned_out, rev_taps, mats, part, packed, arrived,
    load_sem, early_send, early_recv, save_sem, block_send, block_recv, sum_send, sum_recv,
):
    rows, channels = conv_ref.shape
    groups = taps_ref.shape[0]
    size = channels // groups
    per_tile = TILE // size
    tiles = channels // TILE
    half = tiles // 2
    dp, ctx = lax.axis_index("dp"), lax.axis_index("ctx")
    me = dp * 2 + ctx
    share = gkern_ref.shape[1]

    def place(index):
        return {"dp": index // 2, "ctx": lax.rem(index, 2)}

    loads = [
        pltpu.make_async_copy(source, target, load_sem.at[i])
        for i, (source, target) in enumerate(
            [(taps_hbm, taps_ref), (gate_hbm, gate_ref), (grad_hbm, grad_ref), (conv_hbm, conv_ref)]
        )
    ]
    for load in loads:
        load.start()

    barrier = pltpu.get_barrier_semaphore()
    for step in range(1, peers):
        pl.semaphore_signal(barrier, inc=1, device_id=place(lax.rem(me + step, peers)), device_id_type=MESH)

    def columns(first_tile, count):
        return pl.ds(pl.multiple_of(first_tile * TILE, TILE), count * TILE)

    partner = {"ctx": 1 - ctx}

    def early(source, slot):
        return pltpu.make_async_remote_copy(
            src_ref=source.at[:, columns((1 - ctx) * half, half)], dst_ref=early_in.at[slot],
            send_sem=early_send.at[slot], recv_sem=early_recv.at[slot],
            device_id=partner, device_id_type=MESH,
        )

    pl.semaphore_wait(barrier, peers - 1)

    @pl.when(ctx == 0)
    def _():
        early(conv_hbm, 0).start()

    @pl.when(ctx == 1)
    def _():
        early(gate_hbm, 0).start()
        early(grad_hbm, 1).start()

    row, col = iota((rows, rows), 0), iota((rows, rows), 1)
    upper = (row + col >= rows - 1).astype(F32).astype(BF16)
    beyond = (row + col < rows - 1).astype(F32).astype(BF16)
    backwards = jnp.where(row + col == rows - 1, 1.0, 0.0).astype(BF16)
    wrapped = jnp.where(lax.rem(row + col, rows) == 0, 1.0, 0.0).astype(BF16)
    loads[0].wait()
    rev_taps[0] = dot(taps_ref[:, :rows], wrapped)
    rev_taps[1] = dot(taps_ref[:, rows:], wrapped)

    lane = iota((1, TILE), 1)
    both = lax.rem(iota((1, 2 * TILE), 1), TILE)
    masks = [((lane // size) == q).astype(F32).astype(BF16) for q in range(per_tile)]

    def lanes(tile):
        start = tile * TILE
        return pl.ds(start if isinstance(tile, int) else pl.multiple_of(start, TILE), TILE)

    def bits(mask):
        return mask.astype(F32).astype(BF16)

    strips = rows // STRIP
    strip_row, strip_col = iota((STRIP, rows), 0), iota((STRIP, rows), 1)
    below = [bits(strip_row + n * STRIP >= strip_col) for n in range(strips)]
    above = [bits(strip_row + n * STRIP < strip_col) for n in range(strips)]

    def turn(strip, n):
        return pltpu.roll(strip, n * STRIP, 1) if n else strip

    def build(tile):
        for q in range(per_tile):
            group = pl.ds(tile * per_tile + q, 1)
            near, far = [
                pltpu.roll(
                    jnp.broadcast_to(rev_taps[h, group, :], (STRIP, rows)), 0, 1, stride=1, stride_axis=0
                ).astype(BF16)
                for h in range(2)
            ]
            for n in range(strips):
                at = slice(q * rows + n * STRIP, q * rows + (n + 1) * STRIP)
                near_n, far_n = turn(near, n), turn(far, n)
                mats[tile, at, :rows] = near_n * below[n]
                mats[tile, at, rows:] = far_n * below[n] + near_n * above[n]

    def diagonals(matrix):
        total = jnp.zeros((STRIP, rows), F32)
        for n in range(strips):
            total = total + turn(matrix[n * STRIP : (n + 1) * STRIP], n).astype(F32)
        turned = pltpu.roll(total, 0, 1, stride=1, stride_axis=0)
        return jnp.sum(turned, axis=0, keepdims=True)

    def masked(block):
        return jnp.concatenate([block * m for m in masks], axis=0)

    def pairs(tile):
        return dot_lanes(masked(flipped_x[:, lanes(tile)]), mixed[:, lanes(tile)])

    def near_only(step):
        tile = (1 - ctx) * half + step
        found = pairs(tile).astype(BF16)
        for q in range(per_tile):
            group = pl.ds(tile * per_tile + q, 1)
            part[0, group, :] = diagonals(found[q * rows : (q + 1) * rows] * upper)
            part[1, group, :] = jnp.zeros((1, rows), F32)

    def near_and_far(step):
        tile = ctx * half + step
        found = pairs(tile).astype(BF16)
        own_x, own_g, block = flipped_x[:, lanes(tile)], mixed[:, lanes(tile)], landed[:, lanes(tile)]
        across = dot_lanes(masked(jnp.where(first, own_x, block)), jnp.where(first, block, own_g)).astype(BF16)
        for q in range(per_tile):
            group = pl.ds(tile * per_tile + q, 1)
            inner, outer = found[q * rows : (q + 1) * rows], across[q * rows : (q + 1) * rows]
            part[0, group, :] = diagonals(inner * upper + outer * beyond)
            part[1, group, :] = diagonals(outer * upper)

    for load in loads[1:]:
        load.wait()
    def prepare(at):
        flipped_x[:, at] = dot(backwards, conv_ref[:, at]).astype(BF16)
        mixed[:, at] = (gate_ref[:, at].astype(F32) * grad_ref[:, at].astype(F32)).astype(BF16)

    rest = columns(ctx * half, half)

    def exchange(source):
        return pltpu.make_async_remote_copy(
            src_ref=source.at[:, rest], dst_ref=landed.at[:, rest],
            send_sem=block_send, recv_sem=block_recv,
            device_id=partner, device_id_type=MESH,
        )

    prepare(slice(None))

    @pl.when(ctx == 0)
    def _():
        exchange(flipped_x).start()

    @pl.when(ctx == 1)
    def _():
        exchange(mixed).start()

    for step in range(half):
        near_only(step)

    first = ctx == 0

    @pl.when(ctx == 0)
    def _():
        early(gate_hbm, 0).wait_recv()
        early(grad_hbm, 1).wait_recv()
        landed[:, : half * TILE] = (early_in[0].astype(F32) * early_in[1].astype(F32)).astype(BF16)

    @pl.when(ctx == 1)
    def _():
        early(conv_hbm, 0).wait_recv()
        landed[:, half * TILE :] = dot(backwards, early_in[0]).astype(BF16)

    for step in range(half):
        near_and_far(step)

    for peer in range(peers):
        h, e = peer // (rows // share), peer % (rows // share)
        tile8 = jnp.zeros((8, TILE), F32)
        for j in range(groups // 8):
            value = part[h, 8 * j : 8 * j + 8, :]
            shift = (share * (j - e) + 1) % TILE
            if shift:
                value = pltpu.roll(value, shift, 1)
            tile8 = jnp.where(lane // share == j, value, tile8)
        packed[peer] = tile8

    def send_sum(step):
        peer = lax.rem(me + step, peers)
        return pltpu.make_async_remote_copy(
            src_ref=packed.at[peer], dst_ref=arrived.at[step],
            send_sem=sum_send.at[step], recv_sem=sum_recv.at[step],
            device_id=place(peer), device_id_type=MESH,
        )

    copies = [send_sum(step) for step in range(1, peers)]
    for copy in copies:
        copy.start()

    flipped[...] = dot(backwards, mixed[...]).astype(BF16)
    exchange(mixed).wait_recv()
    turned_block = dot(backwards, landed[...]).astype(BF16)
    zx[...] = jnp.where(first, jnp.zeros_like(turned_block), turned_block)
    zg[...] = jnp.where(first, turned_block, jnp.zeros_like(turned_block))

    def convolve(tile):
        at = lanes(tile)
        stacked = jnp.concatenate(
            [
                jnp.concatenate([conv_ref[:, at], flipped[:, at]], axis=1),
                jnp.concatenate([zx[:, at], zg[:, at]], axis=1),
            ],
            axis=0,
        )
        every = dot(mats[tile], stacked)
        total = every[:rows]
        for q in range(1, per_tile):
            total = jnp.where(both // size == q, every[q * rows : (q + 1) * rows], total)
        convolved = total[:, :TILE]
        out_ref[:, at] = (gate_ref[:, at].astype(F32) * convolved).astype(BF16)
        ggate_ref[:, at] = (grad_ref[:, at].astype(F32) * convolved).astype(BF16)
        turned_out[:, at] = total[:, TILE:].astype(BF16)

    saves = []
    for part_index in range(2):
        for tile in range(part_index * half, (part_index + 1) * half):
            build(tile)
            convolve(tile)
        at = slice(part_index * half * TILE, (part_index + 1) * half * TILE)
        gconv_ref[:, at] = dot(backwards, turned_out[:, at]).astype(BF16)

    exchange(mixed).wait_send()

    @pl.when(ctx == 0)
    def _():
        early(conv_hbm, 0).wait_send()

    @pl.when(ctx == 1)
    def _():
        early(gate_hbm, 0).wait_send()
        early(grad_hbm, 1).wait_send()

    summed = packed[me]
    for step, copy in zip(range(1, peers), copies):
        copy.wait()
        summed = summed + arrived[step]
    summed = summed * scale
    for j in range(groups // 8):
        value = summed if j == 0 else pltpu.roll(summed, TILE - share * j, 1)
        gkern_ref[8 * j : 8 * j + 8, :] = value[:, :share]
    for save in saves:
        save.wait()


def store_kernel(*refs):
    sems = refs[-1]
    copies = [pltpu.make_async_copy(refs[i], refs[4 + i], sems.at[i]) for i in range(4)]
    for copy in copies:
        copy.start()
    for copy in copies:
        copy.wait()


def fused_body(gate_input, conv_input, grad_output, kernel):
    _, rows, channels = conv_input.shape
    groups, lag_count = kernel.shape
    tiles = channels // TILE
    peers = lax.axis_size("dp") * lax.axis_size("ctx")
    scale = 1.0 / math.sqrt(lax.axis_size("dp") * rows * lax.axis_size("ctx"))
    block = jax.ShapeDtypeStruct((rows, channels), BF16)
    vmem = pl.BlockSpec(memory_space=pltpu.VMEM)
    hbm = pl.BlockSpec(memory_space=pltpu.HBM)
    results = pl.pallas_call(
        functools.partial(fused_kernel, peers, scale),
        out_shape=[block, block, block, jax.ShapeDtypeStruct((groups, lag_count // peers), F32)],
        in_specs=[hbm] * 4,
        out_specs=[vmem] * 4,
        scratch_shapes=[pltpu.VMEM((rows, channels), BF16)] * 3
        + [pltpu.VMEM((groups, lag_count), BF16)]
        + [pltpu.VMEM((rows, channels), BF16)] * 4
        + [pltpu.VMEM((2, rows, channels // 2), BF16)]
        + [pltpu.VMEM((rows, channels), BF16)] * 3
        + [
            pltpu.VMEM((2, groups, rows), F32),
            pltpu.VMEM((tiles, (groups // tiles) * rows, 2 * rows), BF16),
            pltpu.VMEM((2, groups, rows), F32),
            pltpu.VMEM((peers, 8, TILE), F32),
            pltpu.VMEM((peers, 8, TILE), F32),
            pltpu.SemaphoreType.DMA((4,)),
            pltpu.SemaphoreType.DMA((2,)),
            pltpu.SemaphoreType.DMA((2,)),
            pltpu.SemaphoreType.DMA((2, 3)),
            pltpu.SemaphoreType.DMA,
            pltpu.SemaphoreType.DMA,
            pltpu.SemaphoreType.DMA((peers,)),
            pltpu.SemaphoreType.DMA((peers,)),
        ],
        compiler_params=pltpu.CompilerParams(
            collective_id=0, has_side_effects=True, vmem_limit_bytes=VMEM_BYTES
        ),
        cost_estimate=pl.CostEstimate(
            flops=20 * rows * rows * channels, bytes_accessed=12 * rows * channels, transcendentals=0
        ),
    )(gate_input[0], conv_input[0], grad_output[0], kernel)
    results = pl.pallas_call(
        store_kernel,
        out_shape=[block, block, block, jax.ShapeDtypeStruct((groups, lag_count // peers), F32)],
        in_specs=[vmem] * 4,
        out_specs=[hbm] * 4,
        scratch_shapes=[pltpu.SemaphoreType.DMA((4,))],
        compiler_params=pltpu.CompilerParams(vmem_limit_bytes=VMEM_BYTES),
    )(*results)
    return (results[0][None], results[1][None], results[2][None], results[3])


def body(gate_input, conv_input, grad_output, kernel):
    _, rows, channels = conv_input.shape
    groups, lag_count = kernel.shape
    peers = lax.axis_size("dp") * lax.axis_size("ctx")
    fits = (
        lax.axis_size("ctx") == 2
        and rows == TILE
        and lag_count == 2 * rows
        and channels % (2 * TILE) == 0
        and TILE % (channels // groups) == 0
        and lag_count % peers == 0
        and rows % (lag_count // peers) == 0
        and groups * (lag_count // peers) == 8 * TILE
    )
    if fits:
        return fused_body(gate_input, conv_input, grad_output, kernel)
    return general_body(gate_input, conv_input, grad_output, kernel)


def solution(mesh):
    return jax.shard_map(
        body,
        mesh=mesh,
        in_specs=(P("dp", "ctx", "ch"), P("dp", "ctx", "ch"), P("dp", "ctx", "ch"), P("ch", None)),
        out_specs=(
            P("dp", "ctx", "ch"),
            P("dp", "ctx", "ch"),
            P("dp", "ctx", "ch"),
            P("ch", ("dp", "ctx")),
        ),
        check_vma=False,
    )
```
